32 devices in a mesh: farm: 2 (over y), clus: 4 (over x, core), lag: 4 (over z).
Axes of the slice: x: 2, y: 2, z: 4, core: 2. Of those that a mesh axis runs over, the one named last changes fastest.
Arguments:
- history: bfloat16 [8, 256, 2048], P(None, ('farm', 'lag'), 'clus'), parts along dimension 1, may hold values from -6 to 6
- kernel: bfloat16 [8, 2048, 2048], P('lag', 'clus'), may hold values from -0.046875 to 0.046875
- moments: bfloat16 [8, 8, 256], P(None, ('farm', 'clus')), parts along dimension 1, may hold values from -6 to 6
- coupling: bfloat16 [4, 3, 8, 256, 256], P('clus', None, 'lag'), may hold values from -0.078125 to 0.078125
- evaluation: float32 [256, 2048], replicated, may hold values from -0.375 to 0.375
- offsets: int32 [8], replicated, may hold values from 0 to 7, as said below
- pair_sources: int32 [4, 3], replicated, may hold values from 0 to 3, as said below
- body_cluster: int32 [128], replicated, may hold values from 0 to 3, as said below
Outputs:
- total: bfloat16 [256, 2048], P(('farm', 'lag'), 'clus'), parts along dimension 0
The draws below stay inside these ranges and needn't reach their ends.
There are 2 independent parts, one for each index of `farm`. The reference program is written for one: setup_inputs(seed, part) draws one part's arguments, and reference() takes and returns one part's arrays. A program takes and returns all parts, laid end to end along the dimension named above; an argument that names none is the same for every part. Nothing has to cross between parts.
Inputs may be any that keep to these rules, and one draw needn't show every extreme that they name: offsets lists every cycle slot exactly once. `pair_sources`: row d lists every cluster other than d exactly once. `body_cluster`: every cluster holds exactly 32 bodies.
All inputs are finite; a program needn't handle non-finite values.
Results may differ from the reference program's by a relative error of at most 0.0015.
Values may be sent and summed in bfloat16 or wider, within the bound.
A program may use at most 64 MiB of HBM per device.

```python
import jax
import jax.numpy as jnp
from jax import lax

P_SIZE = 2048
M = 256
BPC = 32
LAGS = 8
CLUSTERS = 4
NP = 3
BODIES = 128


def draw_offsets(key, part):
    return jax.random.permutation(key, LAGS).astype(jnp.int32)


def draw_pair_sources(key, part):
    keys = jax.random.split(key, CLUSTERS)
    perms = jax.vmap(lambda one: jax.random.permutation(one, CLUSTERS - 1))(keys)
    dest = jnp.arange(CLUSTERS)[:, None]
    return (perms + (perms >= dest)).astype(jnp.int32)


def draw_body_cluster(key, part):
    labels = (jnp.arange(BODIES) // BPC).astype(jnp.int32)
    return jax.random.permutation(key, labels).astype(jnp.int32)


def steps_of(rng, dims, shards, smallest, high):
    factor_of = 1.0
    for axis_at, parts in shards:
        draws = jax.random.uniform(jax.random.fold_in(jax.random.fold_in(rng, 6), axis_at), (parts,), jnp.float32, smallest / len(shards), high / len(shards))
        factor_of = factor_of * jnp.repeat(jnp.exp(draws), dims[axis_at] // parts).reshape((-1,) + (1,) * (len(dims) - 1 - axis_at))
    return factor_of


def normal_values(key, shape, width, limit, shards=(), dtype=jnp.bfloat16):
    result = jax.random.normal(key, shape, jnp.float32) * width
    if len(shards) > 0:
        result = steps_of(key, shape, shards, -0.22, 0.18) * result
    return jnp.clip(result, min=-limit, max=limit).astype(dtype)


def setup_inputs(seed: int = 0, part: int = 0) -> dict:
    seeds = jax.random.split(jax.random.key(seed), 9)
    own_keys = jax.random.split(jax.random.fold_in(seeds[8], part), 9)
    return {
        "history": normal_values(own_keys[0], (LAGS, BODIES, P_SIZE), 1.0, 6.0, ((1, 4), (2, 4))),
        "kernel": normal_values(seeds[1], (LAGS, P_SIZE, P_SIZE), (LAGS * P_SIZE) ** -0.5, 0.046875, ((0, 4), (1, 4))),
        "moments": normal_values(own_keys[2], (LAGS, CLUSTERS, M), 1.0, 6.0, ((1, 4),)),
        "coupling": normal_values(seeds[3], (CLUSTERS, NP, LAGS, M, M), (NP * LAGS * M) ** -0.5, 0.078125, ((0, 4), (2, 4))),
        "evaluation": normal_values(seeds[4], (M, P_SIZE), M ** -0.5, 0.375, (), jnp.float32),
        "offsets": draw_offsets(jax.random.fold_in(seeds[8], 71), part),
        "pair_sources": draw_pair_sources(jax.random.fold_in(seeds[8], 71), part),
        "body_cluster": draw_body_cluster(jax.random.fold_in(seeds[8], 71), part),
    }


def reference(history, kernel, moments, coupling, evaluation, offsets, pair_sources, body_cluster):
    hist_type = jnp.float32

    def lag_step(accum, lag_id):
        slot = offsets[lag_id]
        rows = history[slot].astype(hist_type)
        weights = kernel[lag_id].astype(hist_type)
        return accum + jnp.dot(rows, weights, precision=lax.Precision.HIGHEST), None

    start = jnp.zeros((history.shape[1], history.shape[2]), hist_type)
    self_field, _ = lax.scan(lag_step, start, jnp.arange(offsets.shape[0]).astype(jnp.int32))
    picked = moments[offsets].astype(jnp.float32)

    def one_cluster(index):
        sources = pair_sources[index]
        source_moments = picked[:, sources, :]
        mats = coupling[index].astype(jnp.float32)
        return jnp.einsum('klmn,lkn->m', mats, source_moments, precision=lax.Precision.HIGHEST)

    local = lax.map(one_cluster, jnp.arange(pair_sources.shape[0]).astype(jnp.int32))
    far = jnp.dot(local, evaluation, precision=lax.Precision.HIGHEST)
    total = self_field + far[body_cluster]
    return total.astype(jnp.bfloat16)
```

```python
import functools

import jax
import jax.numpy as jnp
from jax import lax
from jax.experimental import pallas as pl
from jax.experimental.pallas import tpu as pltpu
from jax.sharding import PartitionSpec as P

MESH = pl.DeviceIdType.MESH
F32 = jnp.float32
BF16 = jnp.bfloat16


def flipped(index, bits):
    low, high = lax.rem(index, 2), index // 2
    if bits & 1:
        low = 1 - low
    if bits & 2:
        high = 1 - high
    return high * 2 + low


def body(
    lags, clusters,
    history, kernel, moments, coupling, evaluation, offsets, pair_sources, body_cluster,
    out,
    hist, weights, mats, eval_block,
    own_rows, hist_send, hist_recv,
    core_send, core_recv, row_send, row_recv, lag_send, lag_recv, kept,
    moment_all, part_send, part_recv, local_all, far_rows, far,
    hist_sem, weight_sem, mats_sem, eval_sem,
    hist_sems, core_sems, row_sems, lag_sems, moment_sems, part_sems, local_sems,
):
    farm = lax.axis_index("farm")
    clus = lax.axis_index("clus")
    lag = lax.axis_index("lag")
    bodies, panels = out.shape
    lags_here = kernel.shape[0]
    pairs = coupling.shape[1]

    blocks = [flipped(clus, 3), flipped(clus, 2), flipped(clus, 1), clus]
    hist_in = pltpu.make_async_copy(history, hist, hist_sem)
    hist_in.start()
    weights_in = []
    for quad in range(clusters):
        columns = pl.ds(pl.multiple_of(blocks[quad] * panels, panels), panels)
        weights_in.append(
            pltpu.make_async_copy(
                kernel.at[:, :, columns], weights.at[quad], weight_sem.at[quad]
            )
        )
        weights_in[quad].start()
    mats_in = pltpu.make_async_copy(coupling.at[0], mats, mats_sem)
    mats_in.start()
    my_columns = pl.ds(pl.multiple_of(clus * panels, panels), panels)
    eval_in = pltpu.make_async_copy(evaluation.at[:, my_columns], eval_block, eval_sem)
    eval_in.start()

    lag_peers = [(farm, clus, flipped(lag, j)) for j in range(lags)]
    clus_peers = [(farm, flipped(clus, r), lag) for r in range(clusters)]
    barrier = pltpu.get_barrier_semaphore()
    for peer in lag_peers[1:] + clus_peers[1:]:
        pl.semaphore_signal(barrier, inc=1, device_id=peer, device_id_type=MESH)

    for slot in range(moments.shape[0]):
        moment_all[clus, slot : slot + 1, :] = moments[slot].astype(F32)
    hist_in.wait()
    for l in range(lags_here):
        own_rows[l] = hist[offsets[lag * lags_here + l]]
        for j in range(1, lags):
            hist_send[j - 1, l] = hist[offsets[lag_peers[j][2] * lags_here + l]]
    pl.semaphore_wait(barrier, lags - 1 + clusters - 1)

    sent = []

    def send(src, dst, sems, at, peer):
        copy = pltpu.make_async_remote_copy(
            src_ref=src, dst_ref=dst,
            send_sem=sems.at[(0,) + at], recv_sem=sems.at[(1,) + at],
            device_id=peer, device_id_type=MESH,
        )
        copy.start()
        sent.append(copy)
        return copy

    hist_copies = [
        send(hist_send.at[j - 1], hist_recv.at[j - 1], hist_sems, (j - 1,), lag_peers[j])
        for j in range(1, lags)
    ]
    moment_copies = [
        send(moment_all.at[clus], moment_all.at[clus], moment_sems, (r - 1,), clus_peers[r])
        for r in range(1, clusters)
    ]

    core_copies, row_copies, lag_copies = {}, {}, []

    def product(j, quad):
        rows = own_rows if j == 0 else hist_recv.at[j - 1]
        total = None
        for l in range(lags_here):
            term = jnp.dot(rows[l], weights[quad, l], preferred_element_type=F32)
            total = term if total is None else total + term
        return total

    def begin(j):
        if j > 0:
            hist_copies[j - 1].wait_recv()
        for side, quad in ((0, 0), (1, 2)):
            if j == 0:
                weights_in[quad].wait()
            core_send[j, side] = product(j, quad)
            core_copies[j, side] = send(
                core_send.at[j, side], core_recv.at[j, side], core_sems, (j, side), clus_peers[1]
            )
        if j == 0:
            weights_in[1].wait()
        other = product(j, 1)
        core_copies[j, 0].wait_recv()
        row_send[j] = other + core_recv[j, 0]
        row_copies[j] = send(row_send.at[j], row_recv.at[j], row_sems, (j,), clus_peers[2])
        if j == 0:
            weights_in[3].wait()
        mine = product(j, 3)
        core_copies[j, 1].wait_recv()
        kept[j] = mine + core_recv[j, 1]

    def finish(j):
        row_copies[j].wait_recv()
        if j == 0:
            kept[0] = kept[0] + row_recv[0]
        else:
            lag_send[j - 1] = kept[j] + row_recv[j]
            lag_copies.append(
                send(lag_send.at[j - 1], lag_recv.at[j - 1], lag_sems, (j - 1,), lag_peers[j])
            )

    begin(0)

    mats_in.wait()
    for copy in moment_copies:
        copy.wait_recv()
    part = None
    for l in range(lags_here):
        slot = offsets[lag * lags_here + l]
        for k in range(pairs):
            row = moment_all[pair_sources[clus, k], pl.ds(slot, 1), :]
            row = jnp.broadcast_to(row, (16, row.shape[1])).astype(BF16)
            term = lax.dot_general(
                row, mats[k, l], (((1,), (1,)), ((), ())), preferred_element_type=F32
            )
            part = term if part is None else part + term
    part_send[...] = part[0:8]
    part_copies = [
        send(part_send, part_recv.at[j - 1], part_sems, (j - 1,), lag_peers[j])
        for j in range(1, lags)
    ]

    begin(1)
    finish(0)

    local = part_send[...]
    for j in range(1, lags):
        part_copies[j - 1].wait_recv()
        local = local + part_recv[j - 1]
    local_all[clus] = local
    local_copies = [
        send(local_all.at[clus], local_all.at[clus], local_sems, (r - 1,), clus_peers[r])
        for r in range(1, clusters)
    ]

    begin(2)
    finish(1)
    begin(3)
    finish(2)

    eval_in.wait()
    for copy in local_copies:
        copy.wait_recv()
    expansions = local_all[...].reshape(clusters * 8, local_all.shape[2])
    far_rows[...] = jnp.dot(
        expansions, eval_block[...], precision=lax.Precision.HIGHEST, preferred_element_type=F32
    )
    for b in range(bodies):
        far[b : b + 1, :] = far_rows[pl.ds(body_cluster[lag * bodies + b] * 8, 1), :]

    finish(3)
    total = kept[0]
    for j in range(1, lags):
        lag_copies[j - 1].wait_recv()
        total = total + lag_recv[j - 1]
    out[...] = (total + far[...]).astype(BF16)
    for copy in sent:
        copy.wait_send()


def shards_kernel(lags, clusters, history, kernel, moments, coupling, evaluation, offsets, pair_sources, body_cluster):
    slots, bodies, panels = history.shape
    lags_here, depth, _ = kernel.shape
    terms = moments.shape[2]
    pairs = coupling.shape[1]
    dma = pltpu.SemaphoreType.DMA
    anywhere = pl.BlockSpec(memory_space=pl.ANY)
    vmem = pl.BlockSpec(memory_space=pltpu.VMEM)
    smem = pl.BlockSpec(memory_space=pltpu.SMEM)
    block = (bodies, panels)
    flops = 2 * lags * bodies * lags_here * depth * clusters * panels
    return pl.pallas_call(
        functools.partial(body, lags, clusters),
        out_shape=jax.ShapeDtypeStruct(block, BF16),
        in_specs=[anywhere, anywhere, vmem, anywhere, anywhere, smem, smem, smem],
        out_specs=vmem,
        scratch_shapes=[
            pltpu.VMEM((slots,) + block, BF16),
            pltpu.VMEM((clusters, lags_here, depth, panels), BF16),
            pltpu.VMEM((pairs, lags_here, terms, terms), BF16),
            pltpu.VMEM((terms, panels), F32),
            pltpu.VMEM((lags_here,) + block, BF16),
            pltpu.VMEM((lags - 1, lags_here) + block, BF16),
            pltpu.VMEM((lags - 1, lags_here) + block, BF16),
            pltpu.VMEM((lags, 2) + block, F32),
            pltpu.VMEM((lags, 2) + block, F32),
            pltpu.VMEM((lags,) + block, F32),
            pltpu.VMEM((lags,) + block, F32),
            pltpu.VMEM((lags - 1,) + block, F32),
            pltpu.VMEM((lags - 1,) + block, F32),
            pltpu.VMEM((lags,) + block, F32),
            pltpu.VMEM((clusters, slots, terms), F32),
            pltpu.VMEM((8, terms), F32),
            pltpu.VMEM((lags - 1, 8, terms), F32),
            pltpu.VMEM((clusters, 8, terms), F32),
            pltpu.VMEM((clusters * 8, panels), F32),
            pltpu.VMEM(block, F32),
            dma, dma((clusters,)), dma, dma,
            dma((2, lags - 1)), dma((2, lags, 2)), dma((2, lags)), dma((2, lags - 1)),
            dma((2, clusters - 1)), dma((2, lags - 1)), dma((2, clusters - 1)),
        ],
        compiler_params=pltpu.CompilerParams(
            collective_id=0, has_side_effects=True, vmem_limit_bytes=48 * 1024 * 1024
        ),
        cost_estimate=pl.CostEstimate(
            flops=flops, bytes_accessed=2 * kernel.size, transcendentals=0
        ),
    )(history, kernel, moments, coupling, evaluation, offsets, pair_sources, body_cluster)


def shards_general(history, kernel, moments, coupling, evaluation, offsets, pair_sources, body_cluster):
    lag_index = lax.axis_index("lag")
    clus_index = lax.axis_index("clus")
    clus_count = lax.axis_size("clus")
    lags_here = kernel.shape[0]
    panel_block = history.shape[2]
    body_block = history.shape[1]
    picked = jnp.take(history, offsets, axis=0)
    arrived = lax.all_to_all(picked, "lag", split_axis=0, concat_axis=1, tiled=True)
    partial_value = jnp.einsum("lbp,lpq->bq", arrived, kernel, preferred_element_type=jnp.float32)
    my_lags = lag_index * lags_here + jnp.arange(lags_here)
    my_slots = jnp.take(offsets, my_lags, axis=0)
    wanted = jnp.take(moments, my_slots, axis=0)
    source_row = lax.dynamic_index_in_dim(pair_sources, clus_index, 0, keepdims=False)
    piece = lax.all_gather(wanted, "clus", axis=1, tiled=True)
    count = piece.shape[1]
    hits = (source_row[:, None] == jnp.arange(count)[None, :]).astype(jnp.float32)
    gathered = jnp.einsum("kn,lnm->klm", hits, piece.astype(jnp.float32))
    selected = gathered.astype(jnp.bfloat16)
    local_part = jnp.einsum(
        "klmn,kln->m", coupling[0], selected, preferred_element_type=jnp.float32
    )
    owned_rows = lax.psum_scatter(partial_value, "lag", scatter_dimension=0, tiled=True)
    owned = lax.psum_scatter(owned_rows, "clus", scatter_dimension=1, tiled=True)
    cluster_ids = jnp.arange(clus_count)
    placed = (cluster_ids == clus_index).astype(jnp.float32)[:, None] * local_part[None, :]
    expansion_all = lax.psum(placed, ("clus", "lag"))
    eval_block = lax.dynamic_slice_in_dim(evaluation, clus_index * panel_block, panel_block, 1)
    far_block = jnp.dot(expansion_all, eval_block, precision=lax.Precision.HIGHEST)
    my_clusters = lax.dynamic_slice_in_dim(body_cluster, lag_index * body_block, body_block, 0)
    chooser = (my_clusters[:, None] == cluster_ids[None, :]).astype(jnp.float32)
    owned = owned + jnp.dot(chooser, far_block, precision=lax.Precision.HIGHEST)
    return owned.astype(jnp.bfloat16)


def solution(mesh):
    in_specs = (
        P(None, ("farm", "lag"), "clus"),
        P("lag", "clus", None),
        P(None, ("farm", "clus"), None),
        P("clus", None, "lag", None, None),
        P(),
        P(),
        P(),
        P(),
    )
    out_specs = P(("farm", "lag"), "clus")
    lags, clusters = mesh.shape["lag"], mesh.shape["clus"]
    if lags == 4 and clusters == 4:
        shards = functools.partial(shards_kernel, lags, clusters)
    else:
        shards = shards_general
    return jax.shard_map(shards, mesh=mesh, in_specs=in_specs, out_specs=out_specs, check_vma=False)
```

```python
import functools

import jax
import jax.numpy as jnp
from jax import lax
from jax.experimental import pallas as pl
from jax.experimental.pallas import tpu as pltpu
from jax.sharding import PartitionSpec as P

MESH = pl.DeviceIdType.MESH
F32 = jnp.float32
BF16 = jnp.bfloat16


def flipped(index, bits):
    low, high = lax.rem(index, 2), index // 2
    if bits & 1:
        low = 1 - low
    if bits & 2:
        high = 1 - high
    return high * 2 + low


def body(
    lags, clusters,
    history, kernel, moments, coupling, evaluation, offsets, pair_sources, body_cluster,
    out,
    hist, weights, mats, eval_block,
    own_rows, hist_send, hist_recv,
    core_send, core_recv, row_send, row_recv, lag_send, lag_recv, kept,
    moment_all, part_send, part_recv, local_all, far_rows, far,
    hist_sem, weight_sem, mats_sem, eval_sem,
    hist_sems, core_sems, row_sems, lag_sems, moment_sems, part_sems, local_sems,
):
    farm = lax.axis_index("farm")
    clus = lax.axis_index("clus")
    lag = lax.axis_index("lag")
    bodies, panels = out.shape
    lags_here = kernel.shape[0]
    pairs = coupling.shape[1]

    blocks = [flipped(clus, 3), flipped(clus, 2), flipped(clus, 1), clus]
    hist_in = pltpu.make_async_copy(history, hist, hist_sem)
    hist_in.start()
    weights_in = []
    for quad in range(clusters):
        columns = pl.ds(pl.multiple_of(blocks[quad] * panels, panels), panels)
        weights_in.append(
            pltpu.make_async_copy(
                kernel.at[:, :, columns], weights.at[quad], weight_sem.at[quad]
            )
        )
        weights_in[quad].start()
    mats_in = pltpu.make_async_copy(coupling.at[0], mats, mats_sem)
    mats_in.start()
    my_columns = pl.ds(pl.multiple_of(clus * panels, panels), panels)
    eval_in = pltpu.make_async_copy(evaluation.at[:, my_columns], eval_block, eval_sem)
    eval_in.start()

    lag_peers = [(farm, clus, flipped(lag, j)) for j in range(lags)]
    clus_peers = [(farm, flipped(clus, r), lag) for r in range(clusters)]
    barrier = pltpu.get_barrier_semaphore()
    for peer in lag_peers[1:] + clus_peers[1:]:
        pl.semaphore_signal(barrier, inc=1, device_id=peer, device_id_type=MESH)

    moment_all[clus] = moments[...].astype(F32)
    hist_in.wait()
    for l in range(lags_here):
        own_rows[l] = hist[offsets[lag * lags_here + l]]
        for j in range(1, lags):
            hist_send[j - 1, l] = hist[offsets[lag_peers[j][2] * lags_here + l]]
    pl.semaphore_wait(barrier, lags - 1 + clusters - 1)

    sent = []

    def send(src, dst, sems, at, peer):
        copy = pltpu.make_async_remote_copy(
            src_ref=src, dst_ref=dst,
            send_sem=sems.at[(0,) + at], recv_sem=sems.at[(1,) + at],
            device_id=peer, device_id_type=MESH,
        )
        copy.start()
        sent.append(copy)
        return copy

    hist_copies = [
        send(hist_send.at[j - 1], hist_recv.at[j - 1], hist_sems, (j - 1,), lag_peers[j])
        for j in range(1, lags)
    ]
    moment_copies = [
        send(moment_all.at[clus], moment_all.at[clus], moment_sems, (r - 1,), clus_peers[r])
        for r in range(1, clusters)
    ]

    core_copies, row_copies, lag_copies = {}, {}, []

    def product(j, quad):
        rows = own_rows if j == 0 else hist_recv.at[j - 1]
        total = None
        for l in range(lags_here):
            term = jnp.dot(rows[l], weights[quad, l], preferred_element_type=F32)
            total = term if total is None else total + term
        return total

    def begin(j):
        if j > 0:
            hist_copies[j - 1].wait_recv()
        for side, quad in ((0, 0), (1, 2)):
            if j == 0:
                weights_in[quad].wait()
            core_send[j, side] = product(j, quad)
            core_copies[j, side] = send(
                core_send.at[j, side], core_recv.at[j, side], core_sems, (j, side), clus_peers[1]
            )
        if j == 0:
            weights_in[1].wait()
        other = product(j, 1)
        core_copies[j, 0].wait_recv()
        row_send[j] = other + core_recv[j, 0]
        row_copies[j] = send(row_send.at[j], row_recv.at[j], row_sems, (j,), clus_peers[2])
        if j == 0:
            weights_in[3].wait()
        mine = product(j, 3)
        core_copies[j, 1].wait_recv()
        kept[j] = mine + core_recv[j, 1]

    def finish(j):
        row_copies[j].wait_recv()
        if j == 0:
            kept[0] = kept[0] + row_recv[0]
        else:
            lag_send[j - 1] = kept[j] + row_recv[j]
            lag_copies.append(
                send(lag_send.at[j - 1], lag_recv.at[j - 1], lag_sems, (j - 1,), lag_peers[j])
            )

    begin(0)

    mats_in.wait()
    for copy in moment_copies:
        copy.wait_recv()
    part = None
    for l in range(lags_here):
        slot = offsets[lag * lags_here + l]
        for k in range(pairs):
            row = moment_all[pair_sources[clus, k], pl.ds(slot, 1), :]
            row = jnp.broadcast_to(row, (16, row.shape[1])).astype(BF16)
            term = lax.dot_general(
                row, mats[k, l], (((1,), (1,)), ((), ())), preferred_element_type=F32
            )
            part = term if part is None else part + term
    part_send[...] = part[0:8]
    part_copies = [
        send(part_send, part_recv.at[j - 1], part_sems, (j - 1,), lag_peers[j])
        for j in range(1, lags)
    ]

    begin(1)
    finish(0)

    local = part_send[...]
    for j in range(1, lags):
        part_copies[j - 1].wait_recv()
        local = local + part_recv[j - 1]
    local_all[clus] = local
    local_copies = [
        send(local_all.at[clus], local_all.at[clus], local_sems, (r - 1,), clus_peers[r])
        for r in range(1, clusters)
    ]

    begin(2)
    finish(1)
    begin(3)
    finish(2)

    eval_in.wait()
    for copy in local_copies:
        copy.wait_recv()
    expansions = local_all[...].reshape(clusters * 8, local_all.shape[2])
    far_rows[...] = jnp.dot(
        expansions, eval_block[...], precision=lax.Precision.HIGHEST, preferred_element_type=F32
    )
    for b in range(bodies):
        far[b : b + 1, :] = far_rows[pl.ds(body_cluster[lag * bodies + b] * 8, 1), :]

    finish(3)
    total = kept[0]
    for j in range(1, lags):
        lag_copies[j - 1].wait_recv()
        total = total + lag_recv[j - 1]
    out[...] = (total + far[...]).astype(BF16)
    for copy in sent:
        copy.wait_send()


def shards_kernel(lags, clusters, history, kernel, moments, coupling, evaluation, offsets, pair_sources, body_cluster):
    slots, bodies, panels = history.shape
    lags_here, depth, _ = kernel.shape
    terms = moments.shape[2]
    moments = moments.reshape(slots, terms)
    pairs = coupling.shape[1]
    dma = pltpu.SemaphoreType.DMA
    anywhere = pl.BlockSpec(memory_space=pl.ANY)
    vmem = pl.BlockSpec(memory_space=pltpu.VMEM)
    smem = pl.BlockSpec(memory_space=pltpu.SMEM)
    block = (bodies, panels)
    flops = 2 * lags * bodies * lags_here * depth * clusters * panels
    return pl.pallas_call(
        functools.partial(body, lags, clusters),
        out_shape=jax.ShapeDtypeStruct(block, BF16),
        in_specs=[anywhere, anywhere, vmem, anywhere, anywhere, smem, smem, smem],
        out_specs=vmem,
        scratch_shapes=[
            pltpu.VMEM((slots,) + block, BF16),
            pltpu.VMEM((clusters, lags_here, depth, panels), BF16),
            pltpu.VMEM((pairs, lags_here, terms, terms), BF16),
            pltpu.VMEM((terms, panels), F32),
            pltpu.VMEM((lags_here,) + block, BF16),
            pltpu.VMEM((lags - 1, lags_here) + block, BF16),
            pltpu.VMEM((lags - 1, lags_here) + block, BF16),
            pltpu.VMEM((lags, 2) + block, F32),
            pltpu.VMEM((lags, 2) + block, F32),
            pltpu.VMEM((lags,) + block, F32),
            pltpu.VMEM((lags,) + block, F32),
            pltpu.VMEM((lags - 1,) + block, F32),
            pltpu.VMEM((lags - 1,) + block, F32),
            pltpu.VMEM((lags,) + block, F32),
            pltpu.VMEM((clusters, slots, terms), F32),
            pltpu.VMEM((8, terms), F32),
            pltpu.VMEM((lags - 1, 8, terms), F32),
            pltpu.VMEM((clusters, 8, terms), F32),
            pltpu.VMEM((clusters * 8, panels), F32),
            pltpu.VMEM(block, F32),
            dma, dma((clusters,)), dma, dma,
            dma((2, lags - 1)), dma((2, lags, 2)), dma((2, lags)), dma((2, lags - 1)),
            dma((2, clusters - 1)), dma((2, lags - 1)), dma((2, clusters - 1)),
        ],
        compiler_params=pltpu.CompilerParams(
            collective_id=0, has_side_effects=True, vmem_limit_bytes=63 * 1024 * 1024
        ),
        cost_estimate=pl.CostEstimate(
            flops=flops, bytes_accessed=2 * kernel.size, transcendentals=0
        ),
    )(history, kernel, moments, coupling, evaluation, offsets, pair_sources, body_cluster)


def shards_general(history, kernel, moments, coupling, evaluation, offsets, pair_sources, body_cluster):
    lag_index = lax.axis_index("lag")
    clus_index = lax.axis_index("clus")
    clus_count = lax.axis_size("clus")
    lags_here = kernel.shape[0]
    panel_block = history.shape[2]
    body_block = history.shape[1]
    picked = jnp.take(history, offsets, axis=0)
    arrived = lax.all_to_all(picked, "lag", split_axis=0, concat_axis=1, tiled=True)
    partial_value = jnp.einsum("lbp,lpq->bq", arrived, kernel, preferred_element_type=jnp.float32)
    my_lags = lag_index * lags_here + jnp.arange(lags_here)
    my_slots = jnp.take(offsets, my_lags, axis=0)
    wanted = jnp.take(moments, my_slots, axis=0)
    source_row = lax.dynamic_index_in_dim(pair_sources, clus_index, 0, keepdims=False)
    piece = lax.all_gather(wanted, "clus", axis=1, tiled=True)
    count = piece.shape[1]
    hits = (source_row[:, None] == jnp.arange(count)[None, :]).astype(jnp.float32)
    gathered = jnp.einsum("kn,lnm->klm", hits, piece.astype(jnp.float32))
    selected = gathered.astype(jnp.bfloat16)
    local_part = jnp.einsum(
        "klmn,kln->m", coupling[0], selected, preferred_element_type=jnp.float32
    )
    owned_rows = lax.psum_scatter(partial_value, "lag", scatter_dimension=0, tiled=True)
    owned = lax.psum_scatter(owned_rows, "clus", scatter_dimension=1, tiled=True)
    cluster_ids = jnp.arange(clus_count)
    placed = (cluster_ids == clus_index).astype(jnp.float32)[:, None] * local_part[None, :]
    expansion_all = lax.psum(placed, ("clus", "lag"))
    eval_block = lax.dynamic_slice_in_dim(evaluation, clus_index * panel_block, panel_block, 1)
    far_block = jnp.dot(expansion_all, eval_block, precision=lax.Precision.HIGHEST)
    my_clusters = lax.dynamic_slice_in_dim(body_cluster, lag_index * body_block, body_block, 0)
    chooser = (my_clusters[:, None] == cluster_ids[None, :]).astype(jnp.float32)
    owned = owned + jnp.dot(chooser, far_block, precision=lax.Precision.HIGHEST)
    return owned.astype(jnp.bfloat16)


def solution(mesh):
    in_specs = (
        P(None, ("farm", "lag"), "clus"),
        P("lag", "clus", None),
        P(None, ("farm", "clus"), None),
        P("clus", None, "lag", None, None),
        P(),
        P(),
        P(),
        P(),
    )
    out_specs = P(("farm", "lag"), "clus")
    lags, clusters = mesh.shape["lag"], mesh.shape["clus"]
    if lags == 4 and clusters == 4:
        shards = functools.partial(shards_kernel, lags, clusters)
    else:
        shards = shards_general
    return jax.shard_map(shards, mesh=mesh, in_specs=in_specs, out_specs=out_specs, check_vma=False)
```

```python
import functools

import jax
import jax.numpy as jnp
from jax import lax
from jax.experimental import pallas as pl
from jax.experimental.pallas import tpu as pltpu
from jax.sharding import PartitionSpec as P

MESH = pl.DeviceIdType.MESH
F32 = jnp.float32
BF16 = jnp.bfloat16


def flipped(index, bits):
    low, high = lax.rem(index, 2), index // 2
    if bits & 1:
        low = 1 - low
    if bits & 2:
        high = 1 - high
    return high * 2 + low


def spread(tile, shape):
    column = jnp.concatenate([tile] * (shape[0] // 8), axis=0)
    return jnp.concatenate([column] * (shape[1] // 128), axis=1)


def encode(values, codes, scales):
    rows, columns = values.shape
    size = jnp.abs(values)
    peak = None
    for i in range(rows // 8):
        for j in range(columns // 128):
            part = size[8 * i : 8 * i + 8, 128 * j : 128 * j + 128]
            peak = part if peak is None else jnp.maximum(peak, part)
    peak = jnp.maximum(peak, 1e-33)
    scales[...] = peak * (1.0 / 32767.0)
    scaled = jnp.round(values * spread(32767.0 / peak, values.shape))
    codes[...] = scaled.astype(jnp.int32).astype(jnp.int16)


def decode(codes, scales):
    return codes[...].astype(jnp.int32).astype(F32) * spread(scales[...], codes.shape)


def body(
    lags, clusters,
    history, kernel, moments, coupling, evaluation, offsets, pair_sources, body_cluster,
    out,
    hist, weights, mats, eval_block,
    own_rows, hist_send, hist_recv,
    core_send, core_recv, row_send, row_recv, row_scale, row_scaled, lag_send, lag_recv, lag_scale, lag_scaled, kept,
    moment_all, part_send, part_recv, local_all, far_rows, far,
    hist_sem, weight_sem, mats_sem, eval_sem,
    hist_sems, core_sems, row_sems, lag_sems, row_scale_sems, lag_scale_sems, moment_sems, part_sems, local_sems,
):
    farm = lax.axis_index("farm")
    clus = lax.axis_index("clus")
    lag = lax.axis_index("lag")
    bodies, panels = out.shape
    lags_here = kernel.shape[0]
    pairs = coupling.shape[1]

    blocks = [flipped(clus, 3), flipped(clus, 2), flipped(clus, 1), clus]
    hist_in = pltpu.make_async_copy(history, hist, hist_sem)
    hist_in.start()
    weights_in = []
    for quad in range(clusters):
        columns = pl.ds(pl.multiple_of(blocks[quad] * panels, panels), panels)
        weights_in.append(
            pltpu.make_async_copy(
                kernel.at[:, :, columns], weights.at[quad], weight_sem.at[quad]
            )
        )
        weights_in[quad].start()
    mats_in = pltpu.make_async_copy(coupling.at[0], mats, mats_sem)
    mats_in.start()
    my_columns = pl.ds(pl.multiple_of(clus * panels, panels), panels)
    eval_in = pltpu.make_async_copy(evaluation.at[:, my_columns], eval_block, eval_sem)
    eval_in.start()

    lag_peers = [(farm, clus, flipped(lag, j)) for j in range(lags)]
    clus_peers = [(farm, flipped(clus, r), lag) for r in range(clusters)]
    barrier = pltpu.get_barrier_semaphore()
    for peer in lag_peers[1:] + clus_peers[1:]:
        pl.semaphore_signal(barrier, inc=1, device_id=peer, device_id_type=MESH)

    moment_all[clus] = moments[...].astype(F32)
    hist_in.wait()
    for l in range(lags_here):
        own_rows[l] = hist[offsets[lag * lags_here + l]]
        for j in range(1, lags):
            hist_send[j - 1, l] = hist[offsets[lag_peers[j][2] * lags_here + l]]
    pl.semaphore_wait(barrier, lags - 1 + clusters - 1)

    sent = []

    def send(src, dst, sems, at, peer):
        copy = pltpu.make_async_remote_copy(
            src_ref=src, dst_ref=dst,
            send_sem=sems.at[(0,) + at], recv_sem=sems.at[(1,) + at],
            device_id=peer, device_id_type=MESH,
        )
        copy.start()
        sent.append(copy)
        return copy

    def send_history(j):
        return send(hist_send.at[j - 1], hist_recv.at[j - 1], hist_sems, (j - 1,), lag_peers[j])

    hist_copies = {j: send_history(j) for j in (2, 1)}
    moment_copies = [
        send(moment_all.at[clus], moment_all.at[clus], moment_sems, (r - 1,), clus_peers[r])
        for r in range(1, clusters)
    ]

    hist_copies[3] = send_history(3)
    core_copies, row_copies, lag_copies = {}, {}, {}

    def product(j, quad):
        rows = own_rows if j == 0 else hist_recv.at[j - 1]
        total = None
        for l in range(lags_here):
            term = jnp.dot(rows[l], weights[quad, l], preferred_element_type=F32)
            total = term if total is None else total + term
        return total

    def begin(j):
        if j > 0:
            hist_copies[j].wait_recv()
        for side, quad in ((0, 0), (1, 2)):
            if j == 0:
                weights_in[quad].wait()
            core_send[j, side] = product(j, quad)
            core_copies[j, side] = send(
                core_send.at[j, side], core_recv.at[j, side], core_sems, (j, side), clus_peers[1]
            )
        if j == 0:
            weights_in[1].wait()
        other = product(j, 1)
        core_copies[j, 0].wait_recv()
        encode(other + core_recv[j, 0], row_send.at[j], row_scale.at[j])
        row_copies[j] = (
            send(row_send.at[j], row_recv.at[j], row_sems, (j,), clus_peers[2]),
            send(row_scale.at[j], row_scaled.at[j], row_scale_sems, (j,), clus_peers[2]),
        )
        if j == 0:
            weights_in[3].wait()
        mine = product(j, 3)
        core_copies[j, 1].wait_recv()
        kept[j] = mine + core_recv[j, 1]

    def finish(j):
        for copy in row_copies[j]:
            copy.wait_recv()
        total = kept[j] + decode(row_recv.at[j], row_scaled.at[j])
        if j == 0:
            kept[0] = total
        else:
            i = j - 1
            encode(total, lag_send.at[i], lag_scale.at[i])
            lag_copies[j] = (
                send(lag_send.at[i], lag_recv.at[i], lag_sems, (i,), lag_peers[j]),
                send(lag_scale.at[i], lag_scaled.at[i], lag_scale_sems, (i,), lag_peers[j]),
            )

    begin(0)

    mats_in.wait()
    for copy in moment_copies:
        copy.wait_recv()
    part = None
    for l in range(lags_here):
        slot = offsets[lag * lags_here + l]
        for k in range(pairs):
            row = moment_all[pair_sources[clus, k], pl.ds(slot, 1), :]
            row = jnp.broadcast_to(row, (16, row.shape[1])).astype(BF16)
            term = lax.dot_general(
                row, mats[k, l], (((1,), (1,)), ((), ())), preferred_element_type=F32
            )
            part = term if part is None else part + term
    part_send[...] = part[0:8]
    part_copies = [
        send(part_send, part_recv.at[j - 1], part_sems, (j - 1,), lag_peers[j])
        for j in range(1, lags)
    ]

    begin(1)
    finish(0)

    local = part_send[...]
    for j in range(1, lags):
        part_copies[j - 1].wait_recv()
        local = local + part_recv[j - 1]
    local_all[clus] = local
    local_copies = [
        send(local_all.at[clus], local_all.at[clus], local_sems, (r - 1,), clus_peers[r])
        for r in range(1, clusters)
    ]

    begin(2)
    finish(1)

    eval_in.wait()
    for copy in local_copies:
        copy.wait_recv()
    expansions = local_all[...].reshape(clusters * 8, local_all.shape[2])
    far_rows[...] = jnp.dot(
        expansions, eval_block[...], precision=lax.Precision.HIGHEST, preferred_element_type=F32
    )
    for b in range(bodies):
        far[b : b + 1, :] = far_rows[pl.ds(body_cluster[lag * bodies + b] * 8, 1), :]

    finish(2)
    begin(3)
    finish(3)
    total = kept[0]
    for j in range(1, lags):
        for copy in lag_copies[j]:
            copy.wait_recv()
        total = total + decode(lag_recv.at[j - 1], lag_scaled.at[j - 1])
    out[...] = (total + far[...]).astype(BF16)
    for copy in sent:
        copy.wait_send()


def shards_kernel(lags, clusters, history, kernel, moments, coupling, evaluation, offsets, pair_sources, body_cluster):
    slots, bodies, panels = history.shape
    lags_here, depth, _ = kernel.shape
    terms = moments.shape[2]
    moments = moments.reshape(slots, terms)
    pairs = coupling.shape[1]
    dma = pltpu.SemaphoreType.DMA
    anywhere = pl.BlockSpec(memory_space=pl.ANY)
    vmem = pl.BlockSpec(memory_space=pltpu.VMEM)
    smem = pl.BlockSpec(memory_space=pltpu.SMEM)
    block = (bodies, panels)
    flops = 2 * lags * bodies * lags_here * depth * clusters * panels
    return pl.pallas_call(
        functools.partial(body, lags, clusters),
        out_shape=jax.ShapeDtypeStruct(block, BF16),
        in_specs=[anywhere, anywhere, vmem, anywhere, anywhere, smem, smem, smem],
        out_specs=vmem,
        scratch_shapes=[
            pltpu.VMEM((slots,) + block, BF16),
            pltpu.VMEM((clusters, lags_here, depth, panels), BF16),
            pltpu.VMEM((pairs, lags_here, terms, terms), BF16),
            pltpu.VMEM((terms, panels), F32),
            pltpu.VMEM((lags_here,) + block, BF16),
            pltpu.VMEM((lags - 1, lags_here) + block, BF16),
            pltpu.VMEM((lags - 1, lags_here) + block, BF16),
            pltpu.VMEM((lags, 2) + block, F32),
            pltpu.VMEM((lags, 2) + block, F32),
            pltpu.VMEM((lags,) + block, jnp.int16),
            pltpu.VMEM((lags,) + block, jnp.int16),
            pltpu.VMEM((lags, 8, 128), F32),
            pltpu.VMEM((lags, 8, 128), F32),
            pltpu.VMEM((lags - 1,) + block, jnp.int16),
            pltpu.VMEM((lags - 1,) + block, jnp.int16),
            pltpu.VMEM((lags - 1, 8, 128), F32),
            pltpu.VMEM((lags - 1, 8, 128), F32),
            pltpu.VMEM((lags,) + block, F32),
            pltpu.VMEM((clusters, slots, terms), F32),
            pltpu.VMEM((8, terms), F32),
            pltpu.VMEM((lags - 1, 8, terms), F32),
            pltpu.VMEM((clusters, 8, terms), F32),
            pltpu.VMEM((clusters * 8, panels), F32),
            pltpu.VMEM(block, F32),
            dma, dma((clusters,)), dma, dma,
            dma((2, lags - 1)), dma((2, lags, 2)), dma((2, lags)), dma((2, lags - 1)),
            dma((2, lags)), dma((2, lags - 1)),
            dma((2, clusters - 1)), dma((2, lags - 1)), dma((2, clusters - 1)),
        ],
        compiler_params=pltpu.CompilerParams(
            collective_id=0, has_side_effects=True, vmem_limit_bytes=63 * 1024 * 1024
        ),
        cost_estimate=pl.CostEstimate(
            flops=flops, bytes_accessed=2 * kernel.size, transcendentals=0
        ),
    )(history, kernel, moments, coupling, evaluation, offsets, pair_sources, body_cluster)


def shards_general(history, kernel, moments, coupling, evaluation, offsets, pair_sources, body_cluster):
    lag_index = lax.axis_index("lag")
    clus_index = lax.axis_index("clus")
    clus_count = lax.axis_size("clus")
    lags_here = kernel.shape[0]
    panel_block = history.shape[2]
    body_block = history.shape[1]
    picked = jnp.take(history, offsets, axis=0)
    arrived = lax.all_to_all(picked, "lag", split_axis=0, concat_axis=1, tiled=True)
    partial_value = jnp.einsum("lbp,lpq->bq", arrived, kernel, preferred_element_type=jnp.float32)
    my_lags = lag_index * lags_here + jnp.arange(lags_here)
    my_slots = jnp.take(offsets, my_lags, axis=0)
    wanted = jnp.take(moments, my_slots, axis=0)
    source_row = lax.dynamic_index_in_dim(pair_sources, clus_index, 0, keepdims=False)
    piece = lax.all_gather(wanted, "clus", axis=1, tiled=True)
    count = piece.shape[1]
    hits = (source_row[:, None] == jnp.arange(count)[None, :]).astype(jnp.float32)
    gathered = jnp.einsum("kn,lnm->klm", hits, piece.astype(jnp.float32))
    selected = gathered.astype(jnp.bfloat16)
    local_part = jnp.einsum(
        "klmn,kln->m", coupling[0], selected, preferred_element_type=jnp.float32
    )
    owned_rows = lax.psum_scatter(partial_value, "lag", scatter_dimension=0, tiled=True)
    owned = lax.psum_scatter(owned_rows, "clus", scatter_dimension=1, tiled=True)
    cluster_ids = jnp.arange(clus_count)
    placed = (cluster_ids == clus_index).astype(jnp.float32)[:, None] * local_part[None, :]
    expansion_all = lax.psum(placed, ("clus", "lag"))
    eval_block = lax.dynamic_slice_in_dim(evaluation, clus_index * panel_block, panel_block, 1)
    far_block = jnp.dot(expansion_all, eval_block, precision=lax.Precision.HIGHEST)
    my_clusters = lax.dynamic_slice_in_dim(body_cluster, lag_index * body_block, body_block, 0)
    chooser = (my_clusters[:, None] == cluster_ids[None, :]).astype(jnp.float32)
    owned = owned + jnp.dot(chooser, far_block, precision=lax.Precision.HIGHEST)
    return owned.astype(jnp.bfloat16)


def solution(mesh):
    in_specs = (
        P(None, ("farm", "lag"), "clus"),
        P("lag", "clus", None),
        P(None, ("farm", "clus"), None),
        P("clus", None, "lag", None, None),
        P(),
        P(),
        P(),
        P(),
    )
    out_specs = P(("farm", "lag"), "clus")
    lags, clusters = mesh.shape["lag"], mesh.shape["clus"]
    if lags == 4 and clusters == 4:
        shards = functools.partial(shards_kernel, lags, clusters)
    else:
        shards = shards_general
    return jax.shard_map(shards, mesh=mesh, in_specs=in_specs, out_specs=out_specs, check_vma=False)
```

```python
import functools

import jax
import jax.numpy as jnp
from jax import lax
from jax.experimental import pallas as pl
from jax.experimental.pallas import tpu as pltpu
from jax.sharding import PartitionSpec as P

MESH = pl.DeviceIdType.MESH
F32 = jnp.float32
BF16 = jnp.bfloat16


def flipped(index, bits):
    low, high = lax.rem(index, 2), index // 2
    if bits & 1:
        low = 1 - low
    if bits & 2:
        high = 1 - high
    return high * 2 + low


def spread(tile, shape):
    column = jnp.concatenate([tile] * (shape[0] // 8), axis=0)
    return jnp.concatenate([column] * (shape[1] // 128), axis=1)


def encode(values, codes, scales):
    rows, columns = values.shape
    size = jnp.abs(values)
    peak = None
    for i in range(rows // 8):
        for j in range(columns // 128):
            part = size[8 * i : 8 * i + 8, 128 * j : 128 * j + 128]
            peak = part if peak is None else jnp.maximum(peak, part)
    peak = jnp.maximum(peak, 1e-33)
    scales[...] = peak * (1.0 / 32767.0)
    scaled = jnp.round(values * spread(32767.0 / peak, values.shape))
    codes[...] = scaled.astype(jnp.int32).astype(jnp.int16)


def decode(codes, scales):
    return codes[...].astype(jnp.int32).astype(F32) * spread(scales[...], codes.shape)


def body(
    lags, clusters,
    history, kernel, moments, coupling, evaluation, offsets, pair_sources, body_cluster,
    out,
    hist, weights, mats, eval_block,
    rows, hist_send,
    core_send, core_recv, row_send, row_recv, row_scale, row_scaled, lag_send, lag_recv, lag_scale, lag_scaled, kept,
    moment_all, part_send, part_recv, local_all, far_rows, far,
    hist_sem, weight_sem, mats_sem, eval_sem,
    hist_sems, core_sems, row_sems, lag_sems, row_scale_sems, lag_scale_sems, moment_sems, part_sems, local_sems,
):
    farm = lax.axis_index("farm")
    clus = lax.axis_index("clus")
    lag = lax.axis_index("lag")
    bodies, panels = out.shape
    lags_here = kernel.shape[0]
    pairs = coupling.shape[1]

    blocks = [flipped(clus, 3), flipped(clus, 2), flipped(clus, 1), clus]
    hist_in = pltpu.make_async_copy(history, hist, hist_sem)
    hist_in.start()
    weights_in = []
    for quad in range(clusters):
        columns = pl.ds(pl.multiple_of(blocks[quad] * panels, panels), panels)
        weights_in.append(
            pltpu.make_async_copy(
                kernel.at[:, :, columns], weights.at[quad], weight_sem.at[quad]
            )
        )
        weights_in[quad].start()
    mats_in = pltpu.make_async_copy(coupling.at[0], mats, mats_sem)
    mats_in.start()
    my_columns = pl.ds(pl.multiple_of(clus * panels, panels), panels)
    eval_in = pltpu.make_async_copy(evaluation.at[:, my_columns], eval_block, eval_sem)
    eval_in.start()

    lag_peers = [(farm, clus, flipped(lag, j)) for j in range(lags)]
    clus_peers = [(farm, flipped(clus, r), lag) for r in range(clusters)]
    barrier = pltpu.get_barrier_semaphore()
    for peer in lag_peers[1:] + clus_peers[1:]:
        pl.semaphore_signal(barrier, inc=1, device_id=peer, device_id_type=MESH)

    moment_all[clus] = moments[...].astype(F32)
    hist_in.wait()
    for l in range(lags_here):
        rows[l, 0:bodies] = hist[offsets[lag * lags_here + l]]
        for j in range(1, lags):
            hist_send[j - 1, l] = hist[offsets[lag_peers[j][2] * lags_here + l]]
    pl.semaphore_wait(barrier, lags - 1 + clusters - 1)

    sent = []

    def send(src, dst, sems, at, peer):
        copy = pltpu.make_async_remote_copy(
            src_ref=src, dst_ref=dst,
            send_sem=sems.at[(0,) + at], recv_sem=sems.at[(1,) + at],
            device_id=peer, device_id_type=MESH,
        )
        copy.start()
        sent.append(copy)
        return copy

    def send_history(j):
        landing = rows.at[:, pl.ds(j * bodies, bodies)]
        return send(hist_send.at[j - 1], landing, hist_sems, (j - 1,), lag_peers[j])

    hist_copies = {j: send_history(j) for j in (2, 1)}
    moment_copies = [
        send(moment_all.at[clus], moment_all.at[clus], moment_sems, (r - 1,), clus_peers[r])
        for r in range(1, clusters)
    ]

    hist_copies[3] = send_history(3)
    core_copies, row_copies, lag_copies = {}, {}, {}

    height = 2 * bodies

    def product(group, quad):
        if group == 0:
            weights_in[quad].wait()
        total = None
        for l in range(lags_here):
            term = jnp.dot(
                rows[l, group * height : (group + 1) * height], weights[quad, l],
                preferred_element_type=F32,
            )
            total = term if total is None else total + term
        return total

    def begin(group):
        for j in (2 * group, 2 * group + 1):
            if j > 0:
                hist_copies[j].wait_recv()
        for side, quad in ((0, 0), (1, 2)):
            core_send[group, side] = product(group, quad)
            core_copies[group, side] = send(
                core_send.at[group, side], core_recv.at[group, side],
                core_sems, (group, side), clus_peers[1],
            )
        other = product(group, 1)
        core_copies[group, 0].wait_recv()
        encode(other + core_recv[group, 0], row_send.at[group], row_scale.at[group])
        row_copies[group] = (
            send(row_send.at[group], row_recv.at[group], row_sems, (group,), clus_peers[2]),
            send(row_scale.at[group], row_scaled.at[group], row_scale_sems, (group,), clus_peers[2]),
        )
        mine = product(group, 3)
        core_copies[group, 1].wait_recv()
        kept[group] = mine + core_recv[group, 1]

    def finish(group):
        for copy in row_copies[group]:
            copy.wait_recv()
        total = kept[group] + decode(row_recv.at[group], row_scaled.at[group])
        if group == 0:
            kept[0] = total
        for j in (2 * group, 2 * group + 1):
            if j > 0:
                i, top = j - 1, (j - 2 * group) * bodies
                encode(total[top : top + bodies], lag_send.at[i], lag_scale.at[i])
                lag_copies[j] = (
                    send(lag_send.at[i], lag_recv.at[i], lag_sems, (i,), lag_peers[j]),
                    send(lag_scale.at[i], lag_scaled.at[i], lag_scale_sems, (i,), lag_peers[j]),
                )

    mats_in.wait()
    for copy in moment_copies:
        copy.wait_recv()
    part = None
    for l in range(lags_here):
        slot = offsets[lag * lags_here + l]
        for k in range(pairs):
            row = moment_all[pair_sources[clus, k], pl.ds(slot, 1), :]
            row = jnp.broadcast_to(row, (16, row.shape[1])).astype(BF16)
            term = lax.dot_general(
                row, mats[k, l], (((1,), (1,)), ((), ())), preferred_element_type=F32
            )
            part = term if part is None else part + term
    part_send[...] = part[0:8]
    part_copies = [
        send(part_send, part_recv.at[j - 1], part_sems, (j - 1,), lag_peers[j])
        for j in range(1, lags)
    ]

    begin(0)

    local = part_send[...]
    for j in range(1, lags):
        part_copies[j - 1].wait_recv()
        local = local + part_recv[j - 1]
    local_all[clus] = local
    local_copies = [
        send(local_all.at[clus], local_all.at[clus], local_sems, (r - 1,), clus_peers[r])
        for r in range(1, clusters)
    ]

    finish(0)

    eval_in.wait()
    for copy in local_copies:
        copy.wait_recv()
    expansions = local_all[...].reshape(clusters * 8, local_all.shape[2])
    far_rows[...] = jnp.dot(
        expansions, eval_block[...], precision=lax.Precision.HIGHEST, preferred_element_type=F32
    )
    for b in range(bodies):
        far[b : b + 1, :] = far_rows[pl.ds(body_cluster[lag * bodies + b] * 8, 1), :]

    begin(1)
    finish(1)
    total = kept[0, 0:bodies]
    for j in range(1, lags):
        for copy in lag_copies[j]:
            copy.wait_recv()
        total = total + decode(lag_recv.at[j - 1], lag_scaled.at[j - 1])
    out[...] = (total + far[...]).astype(BF16)
    for copy in sent:
        copy.wait_send()


def shards_kernel(lags, clusters, history, kernel, moments, coupling, evaluation, offsets, pair_sources, body_cluster):
    slots, bodies, panels = history.shape
    lags_here, depth, _ = kernel.shape
    terms = moments.shape[2]
    moments = moments.reshape(slots, terms)
    pairs = coupling.shape[1]
    dma = pltpu.SemaphoreType.DMA
    anywhere = pl.BlockSpec(memory_space=pl.ANY)
    vmem = pl.BlockSpec(memory_space=pltpu.VMEM)
    smem = pl.BlockSpec(memory_space=pltpu.SMEM)
    block, double, groups = (bodies, panels), (2 * bodies, panels), lags // 2
    flops = 2 * lags * bodies * lags_here * depth * clusters * panels
    return pl.pallas_call(
        functools.partial(body, lags, clusters),
        out_shape=pltpu.VMEM(block, BF16),
        in_specs=[anywhere, anywhere, vmem, anywhere, anywhere, smem, smem, smem],
        out_specs=vmem,
        scratch_shapes=[
            pltpu.VMEM((slots,) + block, BF16),
            pltpu.VMEM((clusters, lags_here, depth, panels), BF16),
            pltpu.VMEM((pairs, lags_here, terms, terms), BF16),
            pltpu.VMEM((terms, panels), F32),
            pltpu.VMEM((lags_here, lags * bodies, panels), BF16),
            pltpu.VMEM((lags - 1, lags_here) + block, BF16),
            pltpu.VMEM((groups, 2) + double, F32),
            pltpu.VMEM((groups, 2) + double, F32),
            pltpu.VMEM((groups,) + double, jnp.int16),
            pltpu.VMEM((groups,) + double, jnp.int16),
            pltpu.VMEM((groups, 8, 128), F32),
            pltpu.VMEM((groups, 8, 128), F32),
            pltpu.VMEM((lags - 1,) + block, jnp.int16),
            pltpu.VMEM((lags - 1,) + block, jnp.int16),
            pltpu.VMEM((lags - 1, 8, 128), F32),
            pltpu.VMEM((lags - 1, 8, 128), F32),
            pltpu.VMEM((groups,) + double, F32),
            pltpu.VMEM((clusters, slots, terms), F32),
            pltpu.VMEM((8, terms), F32),
            pltpu.VMEM((lags - 1, 8, terms), F32),
            pltpu.VMEM((clusters, 8, terms), F32),
            pltpu.VMEM((clusters * 8, panels), F32),
            pltpu.VMEM(block, F32),
            dma, dma((clusters,)), dma, dma,
            dma((2, lags - 1)), dma((2, groups, 2)), dma((2, groups)), dma((2, lags - 1)),
            dma((2, groups)), dma((2, lags - 1)),
            dma((2, clusters - 1)), dma((2, lags - 1)), dma((2, clusters - 1)),
        ],
        compiler_params=pltpu.CompilerParams(
            collective_id=0, has_side_effects=True, vmem_limit_bytes=63 * 1024 * 1024
        ),
        cost_estimate=pl.CostEstimate(
            flops=flops, bytes_accessed=2 * kernel.size, transcendentals=0
        ),
    )(history, kernel, moments, coupling, evaluation, offsets, pair_sources, body_cluster)


def shards_general(history, kernel, moments, coupling, evaluation, offsets, pair_sources, body_cluster):
    lag_index = lax.axis_index("lag")
    clus_index = lax.axis_index("clus")
    clus_count = lax.axis_size("clus")
    lags_here = kernel.shape[0]
    panel_block = history.shape[2]
    body_block = history.shape[1]
    picked = jnp.take(history, offsets, axis=0)
    arrived = lax.all_to_all(picked, "lag", split_axis=0, concat_axis=1, tiled=True)
    partial_value = jnp.einsum("lbp,lpq->bq", arrived, kernel, preferred_element_type=jnp.float32)
    my_lags = lag_index * lags_here + jnp.arange(lags_here)
    my_slots = jnp.take(offsets, my_lags, axis=0)
    wanted = jnp.take(moments, my_slots, axis=0)
    source_row = lax.dynamic_index_in_dim(pair_sources, clus_index, 0, keepdims=False)
    piece = lax.all_gather(wanted, "clus", axis=1, tiled=True)
    count = piece.shape[1]
    hits = (source_row[:, None] == jnp.arange(count)[None, :]).astype(jnp.float32)
    gathered = jnp.einsum("kn,lnm->klm", hits, piece.astype(jnp.float32))
    selected = gathered.astype(jnp.bfloat16)
    local_part = jnp.einsum(
        "klmn,kln->m", coupling[0], selected, preferred_element_type=jnp.float32
    )
    owned_rows = lax.psum_scatter(partial_value, "lag", scatter_dimension=0, tiled=True)
    owned = lax.psum_scatter(owned_rows, "clus", scatter_dimension=1, tiled=True)
    cluster_ids = jnp.arange(clus_count)
    placed = (cluster_ids == clus_index).astype(jnp.float32)[:, None] * local_part[None, :]
    expansion_all = lax.psum(placed, ("clus", "lag"))
    eval_block = lax.dynamic_slice_in_dim(evaluation, clus_index * panel_block, panel_block, 1)
    far_block = jnp.dot(expansion_all, eval_block, precision=lax.Precision.HIGHEST)
    my_clusters = lax.dynamic_slice_in_dim(body_cluster, lag_index * body_block, body_block, 0)
    chooser = (my_clusters[:, None] == cluster_ids[None, :]).astype(jnp.float32)
    owned = owned + jnp.dot(chooser, far_block, precision=lax.Precision.HIGHEST)
    return owned.astype(jnp.bfloat16)


def solution(mesh):
    in_specs = (
        P(None, ("farm", "lag"), "clus"),
        P("lag", "clus", None),
        P(None, ("farm", "clus"), None),
        P("clus", None, "lag", None, None),
        P(),
        P(),
        P(),
        P(),
    )
    out_specs = P(("farm", "lag"), "clus")
    lags, clusters = mesh.shape["lag"], mesh.shape["clus"]
    if lags == 4 and clusters == 4:
        shards = functools.partial(shards_kernel, lags, clusters)
    else:
        shards = shards_general
    return jax.shard_map(shards, mesh=mesh, in_specs=in_specs, out_specs=out_specs, check_vma=False)
```

```python
import functools

import jax
import jax.numpy as jnp
from jax import lax
from jax.experimental import pallas as pl
from jax.experimental.pallas import tpu as pltpu
from jax.sharding import PartitionSpec as P

MESH = pl.DeviceIdType.MESH
F32 = jnp.float32
BF16 = jnp.bfloat16


def flipped(index, bits):
    low, high = lax.rem(index, 2), index // 2
    if bits & 1:
        low = 1 - low
    if bits & 2:
        high = 1 - high
    return high * 2 + low


def spread(tile, shape):
    column = jnp.concatenate([tile] * (shape[0] // 8), axis=0)
    return jnp.concatenate([column] * (shape[1] // 128), axis=1)


def encode(values, codes, scales):
    rows, columns = values.shape
    size = jnp.abs(values)
    peak = None
    for i in range(rows // 8):
        for j in range(columns // 128):
            part = size[8 * i : 8 * i + 8, 128 * j : 128 * j + 128]
            peak = part if peak is None else jnp.maximum(peak, part)
    peak = jnp.maximum(peak, 1e-33)
    scales[...] = peak * (1.0 / 32767.0)
    scaled = jnp.round(values * spread(32767.0 / peak, values.shape))
    codes[...] = scaled.astype(jnp.int32).astype(jnp.int16)


def decode(codes, scales):
    return codes[...].astype(jnp.int32).astype(F32) * spread(scales[...], codes.shape)


def body(
    lags, clusters,
    history, kernel, moments, coupling, evaluation, offsets_in, sources_in, cluster_in,
    out,
    offsets, pair_sources, body_cluster, moment_rows, hist, weights, mats, eval_block,
    rows, hist_send,
    core_send, core_recv, row_send, row_recv, row_scale, row_scaled, lag_send, lag_recv, lag_scale, lag_scaled, kept,
    moment_all, part_send, part_recv, local_all, far_rows, far,
    small_sem, hist_sem, weight_sem, mats_sem, eval_sem,
    hist_sems, core_sems, row_sems, lag_sems, row_scale_sems, lag_scale_sems, moment_sems, part_sems, local_sems,
):
    farm = lax.axis_index("farm")
    clus = lax.axis_index("clus")
    lag = lax.axis_index("lag")
    bodies, panels = out.shape
    lags_here = kernel.shape[0]
    pairs = coupling.shape[1]

    lag_peers = [(farm, clus, flipped(lag, j)) for j in range(lags)]
    clus_peers = [(farm, flipped(clus, r), lag) for r in range(clusters)]
    barrier = pltpu.get_barrier_semaphore()
    for peer in lag_peers[1:] + clus_peers[1:]:
        pl.semaphore_signal(barrier, inc=1, device_id=peer, device_id_type=MESH)

    small = [
        pltpu.make_async_copy(src, dst, small_sem.at[i])
        for i, (src, dst) in enumerate((
            (offsets_in, offsets), (sources_in, pair_sources),
            (cluster_in, body_cluster), (moments, moment_rows),
        ))
    ]
    small[0].start()
    hist_in = pltpu.make_async_copy(history, hist, hist_sem)
    hist_in.start()
    for copy in small[1:]:
        copy.start()
    blocks = [flipped(clus, 3), flipped(clus, 2), flipped(clus, 1), clus]
    weights_in = []
    for quad in range(clusters):
        columns = pl.ds(pl.multiple_of(blocks[quad] * panels, panels), panels)
        weights_in.append(
            pltpu.make_async_copy(
                kernel.at[:, :, columns], weights.at[quad], weight_sem.at[quad]
            )
        )
        weights_in[quad].start()
    mats_in = pltpu.make_async_copy(coupling.at[0], mats, mats_sem)
    mats_in.start()
    my_columns = pl.ds(pl.multiple_of(clus * panels, panels), panels)
    eval_in = pltpu.make_async_copy(evaluation.at[:, my_columns], eval_block, eval_sem)
    eval_in.start()

    small[0].wait()
    hist_in.wait()
    for l in range(lags_here):
        rows[l, 0:bodies] = hist[offsets[lag * lags_here + l]]
        for j in range(1, lags):
            hist_send[j - 1, l] = hist[offsets[lag_peers[j][2] * lags_here + l]]
    small[3].wait()
    moment_all[clus] = moment_rows[...].astype(F32)
    pl.semaphore_wait(barrier, lags - 1 + clusters - 1)

    sent = []

    def send(src, dst, sems, at, peer):
        copy = pltpu.make_async_remote_copy(
            src_ref=src, dst_ref=dst,
            send_sem=sems.at[(0,) + at], recv_sem=sems.at[(1,) + at],
            device_id=peer, device_id_type=MESH,
        )
        copy.start()
        sent.append(copy)
        return copy

    def send_history(j):
        landing = rows.at[:, pl.ds(j * bodies, bodies)]
        return send(hist_send.at[j - 1], landing, hist_sems, (j - 1,), lag_peers[j])

    hist_copies = {j: send_history(j) for j in (2, 1)}
    moment_copies = [
        send(moment_all.at[clus], moment_all.at[clus], moment_sems, (r - 1,), clus_peers[r])
        for r in range(1, clusters)
    ]

    hist_copies[3] = send_history(3)
    core_copies, row_copies, lag_copies = {}, {}, {}

    height = 2 * bodies

    def product(group, quad):
        if group == 0:
            weights_in[quad].wait()
        total = None
        for l in range(lags_here):
            term = jnp.dot(
                rows[l, group * height : (group + 1) * height], weights[quad, l],
                preferred_element_type=F32,
            )
            total = term if total is None else total + term
        return total

    def begin(group):
        for j in (2 * group, 2 * group + 1):
            if j > 0:
                hist_copies[j].wait_recv()
        for side, quad in ((0, 0), (1, 2)):
            core_send[group, side] = product(group, quad)
            core_copies[group, side] = send(
                core_send.at[group, side], core_recv.at[group, side],
                core_sems, (group, side), clus_peers[1],
            )
        other = product(group, 1)
        core_copies[group, 0].wait_recv()
        encode(other + core_recv[group, 0], row_send.at[group], row_scale.at[group])
        row_copies[group] = (
            send(row_send.at[group], row_recv.at[group], row_sems, (group,), clus_peers[2]),
            send(row_scale.at[group], row_scaled.at[group], row_scale_sems, (group,), clus_peers[2]),
        )
        mine = product(group, 3)
        core_copies[group, 1].wait_recv()
        kept[group] = mine + core_recv[group, 1]

    def finish(group):
        for copy in row_copies[group]:
            copy.wait_recv()
        total = kept[group] + decode(row_recv.at[group], row_scaled.at[group])
        if group == 0:
            kept[0] = total
        for j in (2 * group, 2 * group + 1):
            if j > 0:
                i, top = j - 1, (j - 2 * group) * bodies
                encode(total[top : top + bodies], lag_send.at[i], lag_scale.at[i])
                lag_copies[j] = (
                    send(lag_send.at[i], lag_recv.at[i], lag_sems, (i,), lag_peers[j]),
                    send(lag_scale.at[i], lag_scaled.at[i], lag_scale_sems, (i,), lag_peers[j]),
                )

    small[1].wait()
    mats_in.wait()
    for copy in moment_copies:
        copy.wait_recv()
    part = None
    for l in range(lags_here):
        slot = offsets[lag * lags_here + l]
        for k in range(pairs):
            row = moment_all[pair_sources[clus, k], pl.ds(slot, 1), :]
            row = jnp.broadcast_to(row, (16, row.shape[1])).astype(BF16)
            term = lax.dot_general(
                row, mats[k, l], (((1,), (1,)), ((), ())), preferred_element_type=F32
            )
            part = term if part is None else part + term
    part_send[...] = part[0:8]
    part_copies = [
        send(part_send, part_recv.at[j - 1], part_sems, (j - 1,), lag_peers[j])
        for j in range(1, lags)
    ]

    begin(0)

    local = part_send[...]
    for j in range(1, lags):
        part_copies[j - 1].wait_recv()
        local = local + part_recv[j - 1]
    local_all[clus] = local
    local_copies = [
        send(local_all.at[clus], local_all.at[clus], local_sems, (r - 1,), clus_peers[r])
        for r in range(1, clusters)
    ]

    finish(0)

    small[2].wait()
    eval_in.wait()
    for copy in local_copies:
        copy.wait_recv()
    expansions = local_all[...].reshape(clusters * 8, local_all.shape[2])
    far_rows[...] = jnp.dot(
        expansions, eval_block[...], precision=lax.Precision.HIGHEST, preferred_element_type=F32
    )
    for b in range(bodies):
        far[b : b + 1, :] = far_rows[pl.ds(body_cluster[lag * bodies + b] * 8, 1), :]

    begin(1)
    finish(1)
    total = kept[0, 0:bodies]
    for j in range(1, lags):
        for copy in lag_copies[j]:
            copy.wait_recv()
        total = total + decode(lag_recv.at[j - 1], lag_scaled.at[j - 1])
    out[...] = (total + far[...]).astype(BF16)
    for copy in sent:
        copy.wait_send()


def shards_kernel(lags, clusters, history, kernel, moments, coupling, evaluation, offsets, pair_sources, body_cluster):
    slots, bodies, panels = history.shape
    lags_here, depth, _ = kernel.shape
    terms = moments.shape[2]
    moments = moments.reshape(slots, terms)
    pairs = coupling.shape[1]
    dma = pltpu.SemaphoreType.DMA
    anywhere = pl.BlockSpec(memory_space=pl.ANY)
    vmem = pl.BlockSpec(memory_space=pltpu.VMEM)
    block, double, groups = (bodies, panels), (2 * bodies, panels), lags // 2
    flops = 2 * lags * bodies * lags_here * depth * clusters * panels
    return pl.pallas_call(
        functools.partial(body, lags, clusters),
        out_shape=pltpu.VMEM(block, BF16),
        in_specs=[anywhere] * 8,
        out_specs=vmem,
        scratch_shapes=[
            pltpu.SMEM(offsets.shape, jnp.int32),
            pltpu.SMEM(pair_sources.shape, jnp.int32),
            pltpu.SMEM(body_cluster.shape, jnp.int32),
            pltpu.VMEM((slots, terms), BF16),
            pltpu.VMEM((slots,) + block, BF16),
            pltpu.VMEM((clusters, lags_here, depth, panels), BF16),
            pltpu.VMEM((pairs, lags_here, terms, terms), BF16),
            pltpu.VMEM((terms, panels), F32),
            pltpu.VMEM((lags_here, lags * bodies, panels), BF16),
            pltpu.VMEM((lags - 1, lags_here) + block, BF16),
            pltpu.VMEM((groups, 2) + double, F32),
            pltpu.VMEM((groups, 2) + double, F32),
            pltpu.VMEM((groups,) + double, jnp.int16),
            pltpu.VMEM((groups,) + double, jnp.int16),
            pltpu.VMEM((groups, 8, 128), F32),
            pltpu.VMEM((groups, 8, 128), F32),
            pltpu.VMEM((lags - 1,) + block, jnp.int16),
            pltpu.VMEM((lags - 1,) + block, jnp.int16),
            pltpu.VMEM((lags - 1, 8, 128), F32),
            pltpu.VMEM((lags - 1, 8, 128), F32),
            pltpu.VMEM((groups,) + double, F32),
            pltpu.VMEM((clusters, slots, terms), F32),
            pltpu.VMEM((8, terms), F32),
            pltpu.VMEM((lags - 1, 8, terms), F32),
            pltpu.VMEM((clusters, 8, terms), F32),
            pltpu.VMEM((clusters * 8, panels), F32),
            pltpu.VMEM(block, F32),
            dma((4,)), dma, dma((clusters,)), dma, dma,
            dma((2, lags - 1)), dma((2, groups, 2)), dma((2, groups)), dma((2, lags - 1)),
            dma((2, groups)), dma((2, lags - 1)),
            dma((2, clusters - 1)), dma((2, lags - 1)), dma((2, clusters - 1)),
        ],
        compiler_params=pltpu.CompilerParams(
            collective_id=0, has_side_effects=True, vmem_limit_bytes=63 * 1024 * 1024
        ),
        cost_estimate=pl.CostEstimate(
            flops=flops, bytes_accessed=2 * kernel.size, transcendentals=0
        ),
    )(history, kernel, moments, coupling, evaluation, offsets, pair_sources, body_cluster)


def shards_general(history, kernel, moments, coupling, evaluation, offsets, pair_sources, body_cluster):
    lag_index = lax.axis_index("lag")
    clus_index = lax.axis_index("clus")
    clus_count = lax.axis_size("clus")
    lags_here = kernel.shape[0]
    panel_block = history.shape[2]
    body_block = history.shape[1]
    picked = jnp.take(history, offsets, axis=0)
    arrived = lax.all_to_all(picked, "lag", split_axis=0, concat_axis=1, tiled=True)
    partial_value = jnp.einsum("lbp,lpq->bq", arrived, kernel, preferred_element_type=jnp.float32)
    my_lags = lag_index * lags_here + jnp.arange(lags_here)
    my_slots = jnp.take(offsets, my_lags, axis=0)
    wanted = jnp.take(moments, my_slots, axis=0)
    source_row = lax.dynamic_index_in_dim(pair_sources, clus_index, 0, keepdims=False)
    piece = lax.all_gather(wanted, "clus", axis=1, tiled=True)
    count = piece.shape[1]
    hits = (source_row[:, None] == jnp.arange(count)[None, :]).astype(jnp.float32)
    gathered = jnp.einsum("kn,lnm->klm", hits, piece.astype(jnp.float32))
    selected = gathered.astype(jnp.bfloat16)
    local_part = jnp.einsum(
        "klmn,kln->m", coupling[0], selected, preferred_element_type=jnp.float32
    )
    owned_rows = lax.psum_scatter(partial_value, "lag", scatter_dimension=0, tiled=True)
    owned = lax.psum_scatter(owned_rows, "clus", scatter_dimension=1, tiled=True)
    cluster_ids = jnp.arange(clus_count)
    placed = (cluster_ids == clus_index).astype(jnp.float32)[:, None] * local_part[None, :]
    expansion_all = lax.psum(placed, ("clus", "lag"))
    eval_block = lax.dynamic_slice_in_dim(evaluation, clus_index * panel_block, panel_block, 1)
    far_block = jnp.dot(expansion_all, eval_block, precision=lax.Precision.HIGHEST)
    my_clusters = lax.dynamic_slice_in_dim(body_cluster, lag_index * body_block, body_block, 0)
    chooser = (my_clusters[:, None] == cluster_ids[None, :]).astype(jnp.float32)
    owned = owned + jnp.dot(chooser, far_block, precision=lax.Precision.HIGHEST)
    return owned.astype(jnp.bfloat16)


def solution(mesh):
    in_specs = (
        P(None, ("farm", "lag"), "clus"),
        P("lag", "clus", None),
        P(None, ("farm", "clus"), None),
        P("clus", None, "lag", None, None),
        P(),
        P(),
        P(),
        P(),
    )
    out_specs = P(("farm", "lag"), "clus")
    lags, clusters = mesh.shape["lag"], mesh.shape["clus"]
    if lags == 4 and clusters == 4:
        shards = functools.partial(shards_kernel, lags, clusters)
    else:
        shards = shards_general
    return jax.shard_map(shards, mesh=mesh, in_specs=in_specs, out_specs=out_specs, check_vma=False)
```

```python
import functools

import jax
import jax.numpy as jnp
from jax import lax
from jax.experimental import pallas as pl
from jax.experimental.pallas import tpu as pltpu
from jax.sharding import PartitionSpec as P

MESH = pl.DeviceIdType.MESH
F32 = jnp.float32
BF16 = jnp.bfloat16


GROUPS = ((0,), (1, 2), (3,))


def flipped(index, bits):
    low, high = lax.rem(index, 2), index // 2
    if bits & 1:
        low = 1 - low
    if bits & 2:
        high = 1 - high
    return high * 2 + low


def spread(tile, shape):
    column = jnp.concatenate([tile] * (shape[0] // 8), axis=0)
    return jnp.concatenate([column] * (shape[1] // 128), axis=1)


def encode(values, codes, scales):
    rows, columns = values.shape
    size = jnp.abs(values)
    peak = None
    for i in range(rows // 8):
        for j in range(columns // 128):
            part = size[8 * i : 8 * i + 8, 128 * j : 128 * j + 128]
            peak = part if peak is None else jnp.maximum(peak, part)
    peak = jnp.maximum(peak, 1e-33)
    scales[...] = peak * (1.0 / 32767.0)
    scaled = jnp.round(values * spread(32767.0 / peak, values.shape))
    codes[...] = scaled.astype(jnp.int32).astype(jnp.int16)


def decode(codes, scales):
    return codes[...].astype(jnp.int32).astype(F32) * spread(scales[...], codes.shape)


def body(
    lags, clusters,
    history, kernel, moments, coupling, evaluation, offsets_in, sources_in, cluster_in,
    out,
    offsets, pair_sources, body_cluster, moment_rows, hist, weights, mats, eval_block,
    rows, hist_send,
    core_send, core_recv, row_send, row_recv, row_scale, row_scaled, lag_send, lag_recv, lag_scale, lag_scaled, kept,
    moment_all, part_send, part_recv, local_all, far_rows, far,
    small_sem, hist_sem, weight_sem, mats_sem, eval_sem,
    hist_sems, core_sems, row_sems, lag_sems, row_scale_sems, lag_scale_sems, moment_sems, part_sems, local_sems,
):
    farm = lax.axis_index("farm")
    clus = lax.axis_index("clus")
    lag = lax.axis_index("lag")
    bodies, panels = out.shape
    lags_here = kernel.shape[0]
    pairs = coupling.shape[1]

    lag_peers = [(farm, clus, flipped(lag, j)) for j in range(lags)]
    clus_peers = [(farm, flipped(clus, r), lag) for r in range(clusters)]
    barrier = pltpu.get_barrier_semaphore()
    for peer in lag_peers[1:] + clus_peers[1:]:
        pl.semaphore_signal(barrier, inc=1, device_id=peer, device_id_type=MESH)

    small = [
        pltpu.make_async_copy(src, dst, small_sem.at[i])
        for i, (src, dst) in enumerate((
            (offsets_in, offsets), (sources_in, pair_sources),
            (cluster_in, body_cluster), (moments, moment_rows),
        ))
    ]
    small[0].start()
    hist_in = pltpu.make_async_copy(history, hist, hist_sem)
    hist_in.start()
    for copy in small[1:]:
        copy.start()
    blocks = [flipped(clus, 3), flipped(clus, 2), flipped(clus, 1), clus]
    weights_in = []
    for quad in range(clusters):
        columns = pl.ds(pl.multiple_of(blocks[quad] * panels, panels), panels)
        weights_in.append(
            pltpu.make_async_copy(
                kernel.at[:, :, columns], weights.at[quad], weight_sem.at[quad]
            )
        )
        weights_in[quad].start()
    mats_in = pltpu.make_async_copy(coupling.at[0], mats, mats_sem)
    mats_in.start()
    my_columns = pl.ds(pl.multiple_of(clus * panels, panels), panels)
    eval_in = pltpu.make_async_copy(evaluation.at[:, my_columns], eval_block, eval_sem)
    eval_in.start()

    small[0].wait()
    hist_in.wait()
    for l in range(lags_here):
        rows[l, 0:bodies] = hist[offsets[lag * lags_here + l]]
        for j in range(1, lags):
            hist_send[j - 1, l] = hist[offsets[lag_peers[j][2] * lags_here + l]]
    small[3].wait()
    moment_all[clus] = moment_rows[...].astype(F32)
    pl.semaphore_wait(barrier, lags - 1 + clusters - 1)

    sent = []

    def send(src, dst, sems, at, peer):
        copy = pltpu.make_async_remote_copy(
            src_ref=src, dst_ref=dst,
            send_sem=sems.at[(0,) + at], recv_sem=sems.at[(1,) + at],
            device_id=peer, device_id_type=MESH,
        )
        copy.start()
        sent.append(copy)
        return copy

    def send_history(j):
        landing = rows.at[:, pl.ds(j * bodies, bodies)]
        return send(hist_send.at[j - 1], landing, hist_sems, (j - 1,), lag_peers[j])

    hist_copies = {j: send_history(j) for j in (2, 1)}
    moment_copies = [
        send(moment_all.at[clus], moment_all.at[clus], moment_sems, (r - 1,), clus_peers[r])
        for r in range(1, clusters)
    ]

    core_copies, row_copies, lag_copies = {}, {}, {}

    def spans(group):
        return GROUPS[group][0] * bodies, len(GROUPS[group]) * bodies

    def product(group, quad):
        if group == 0:
            weights_in[quad].wait()
        top, height = spans(group)
        total = None
        for l in range(lags_here):
            term = jnp.dot(
                rows[l, top : top + height], weights[quad, l], preferred_element_type=F32
            )
            total = term if total is None else total + term
        return total

    def begin(group):
        for j in GROUPS[group]:
            if j > 0:
                hist_copies[j].wait_recv()
        part = pl.ds(0, spans(group)[1])
        for side, quad in ((0, 0), (1, 2)):
            core_send[group, side, part] = product(group, quad)
            core_copies[group, side] = send(
                core_send.at[group, side, part], core_recv.at[group, side, part],
                core_sems, (group, side), clus_peers[1],
            )
            if group == 0 and side == 0:
                hist_copies[3] = send_history(3)
        other = product(group, 1)
        core_copies[group, 0].wait_recv()
        encode(other + core_recv[group, 0, part], row_send.at[group, part], row_scale.at[group])
        row_copies[group] = (
            send(
                row_send.at[group, part], row_recv.at[group, part],
                row_sems, (group,), clus_peers[2],
            ),
            send(
                row_scale.at[group], row_scaled.at[group],
                row_scale_sems, (group,), clus_peers[2],
            ),
        )
        mine = product(group, 3)
        core_copies[group, 1].wait_recv()
        kept[group, part] = mine + core_recv[group, 1, part]

    def finish(group):
        for copy in row_copies[group]:
            copy.wait_recv()
        part = pl.ds(0, spans(group)[1])
        total = kept[group, part] + decode(row_recv.at[group, part], row_scaled.at[group])
        if group == 0:
            kept[0, part] = total
        for at, j in enumerate(GROUPS[group]):
            if j > 0:
                i, top = j - 1, at * bodies
                encode(total[top : top + bodies], lag_send.at[i], lag_scale.at[i])
                lag_copies[j] = (
                    send(lag_send.at[i], lag_recv.at[i], lag_sems, (i,), lag_peers[j]),
                    send(lag_scale.at[i], lag_scaled.at[i], lag_scale_sems, (i,), lag_peers[j]),
                )

    begin(0)

    small[1].wait()
    mats_in.wait()
    for copy in moment_copies:
        copy.wait_recv()
    part = None
    for l in range(lags_here):
        slot = offsets[lag * lags_here + l]
        for k in range(pairs):
            row = moment_all[pair_sources[clus, k], pl.ds(slot, 1), :]
            row = jnp.broadcast_to(row, (16, row.shape[1])).astype(BF16)
            term = lax.dot_general(
                row, mats[k, l], (((1,), (1,)), ((), ())), preferred_element_type=F32
            )
            part = term if part is None else part + term
    part_send[...] = part[0:8]
    part_copies = [
        send(part_send, part_recv.at[j - 1], part_sems, (j - 1,), lag_peers[j])
        for j in range(1, lags)
    ]

    begin(1)
    finish(0)

    local = part_send[...]
    for j in range(1, lags):
        part_copies[j - 1].wait_recv()
        local = local + part_recv[j - 1]
    local_all[clus] = local
    local_copies = [
        send(local_all.at[clus], local_all.at[clus], local_sems, (r - 1,), clus_peers[r])
        for r in range(1, clusters)
    ]

    finish(1)
    begin(2)
    finish(2)

    small[2].wait()
    eval_in.wait()
    for copy in local_copies:
        copy.wait_recv()
    expansions = local_all[...].reshape(clusters * 8, local_all.shape[2])
    far_rows[...] = jnp.dot(
        expansions, eval_block[...], precision=lax.Precision.HIGHEST, preferred_element_type=F32
    )
    for b in range(bodies):
        far[b : b + 1, :] = far_rows[pl.ds(body_cluster[lag * bodies + b] * 8, 1), :]

    total = kept[0, 0:bodies]
    for j in range(1, lags):
        for copy in lag_copies[j]:
            copy.wait_recv()
        total = total + decode(lag_recv.at[j - 1], lag_scaled.at[j - 1])
    out[...] = (total + far[...]).astype(BF16)
    for copy in sent:
        copy.wait_send()


def shards_kernel(lags, clusters, history, kernel, moments, coupling, evaluation, offsets, pair_sources, body_cluster):
    slots, bodies, panels = history.shape
    lags_here, depth, _ = kernel.shape
    terms = moments.shape[2]
    moments = moments.reshape(slots, terms)
    pairs = coupling.shape[1]
    dma = pltpu.SemaphoreType.DMA
    anywhere = pl.BlockSpec(memory_space=pl.ANY)
    vmem = pl.BlockSpec(memory_space=pltpu.VMEM)
    block, double, groups = (bodies, panels), (2 * bodies, panels), len(GROUPS)
    flops = 2 * lags * bodies * lags_here * depth * clusters * panels
    return pl.pallas_call(
        functools.partial(body, lags, clusters),
        out_shape=pltpu.VMEM(block, BF16),
        in_specs=[anywhere] * 8,
        out_specs=vmem,
        scratch_shapes=[
            pltpu.SMEM(offsets.shape, jnp.int32),
            pltpu.SMEM(pair_sources.shape, jnp.int32),
            pltpu.SMEM(body_cluster.shape, jnp.int32),
            pltpu.VMEM((slots, terms), BF16),
            pltpu.VMEM((slots,) + block, BF16),
            pltpu.VMEM((clusters, lags_here, depth, panels), BF16),
            pltpu.VMEM((pairs, lags_here, terms, terms), BF16),
            pltpu.VMEM((terms, panels), F32),
            pltpu.VMEM((lags_here, lags * bodies, panels), BF16),
            pltpu.VMEM((lags - 1, lags_here) + block, BF16),
            pltpu.VMEM((groups, 2) + double, F32),
            pltpu.VMEM((groups, 2) + double, F32),
            pltpu.VMEM((groups,) + double, jnp.int16),
            pltpu.VMEM((groups,) + double, jnp.int16),
            pltpu.VMEM((groups, 8, 128), F32),
            pltpu.VMEM((groups, 8, 128), F32),
            pltpu.VMEM((lags - 1,) + block, jnp.int16),
            pltpu.VMEM((lags - 1,) + block, jnp.int16),
            pltpu.VMEM((lags - 1, 8, 128), F32),
            pltpu.VMEM((lags - 1, 8, 128), F32),
            pltpu.VMEM((groups,) + double, F32),
            pltpu.VMEM((clusters, slots, terms), F32),
            pltpu.VMEM((8, terms), F32),
            pltpu.VMEM((lags - 1, 8, terms), F32),
            pltpu.VMEM((clusters, 8, terms), F32),
            pltpu.VMEM((clusters * 8, panels), F32),
            pltpu.VMEM(block, F32),
            dma((4,)), dma, dma((clusters,)), dma, dma,
            dma((2, lags - 1)), dma((2, groups, 2)), dma((2, groups)), dma((2, lags - 1)),
            dma((2, groups)), dma((2, lags - 1)),
            dma((2, clusters - 1)), dma((2, lags - 1)), dma((2, clusters - 1)),
        ],
        compiler_params=pltpu.CompilerParams(
            collective_id=0, has_side_effects=True, vmem_limit_bytes=63 * 1024 * 1024
        ),
        cost_estimate=pl.CostEstimate(
            flops=flops, bytes_accessed=2 * kernel.size, transcendentals=0
        ),
    )(history, kernel, moments, coupling, evaluation, offsets, pair_sources, body_cluster)


def shards_general(history, kernel, moments, coupling, evaluation, offsets, pair_sources, body_cluster):
    lag_index = lax.axis_index("lag")
    clus_index = lax.axis_index("clus")
    clus_count = lax.axis_size("clus")
    lags_here = kernel.shape[0]
    panel_block = history.shape[2]
    body_block = history.shape[1]
    picked = jnp.take(history, offsets, axis=0)
    arrived = lax.all_to_all(picked, "lag", split_axis=0, concat_axis=1, tiled=True)
    partial_value = jnp.einsum("lbp,lpq->bq", arrived, kernel, preferred_element_type=jnp.float32)
    my_lags = lag_index * lags_here + jnp.arange(lags_here)
    my_slots = jnp.take(offsets, my_lags, axis=0)
    wanted = jnp.take(moments, my_slots, axis=0)
    source_row = lax.dynamic_index_in_dim(pair_sources, clus_index, 0, keepdims=False)
    piece = lax.all_gather(wanted, "clus", axis=1, tiled=True)
    count = piece.shape[1]
    hits = (source_row[:, None] == jnp.arange(count)[None, :]).astype(jnp.float32)
    gathered = jnp.einsum("kn,lnm->klm", hits, piece.astype(jnp.float32))
    selected = gathered.astype(jnp.bfloat16)
    local_part = jnp.einsum(
        "klmn,kln->m", coupling[0], selected, preferred_element_type=jnp.float32
    )
    owned_rows = lax.psum_scatter(partial_value, "lag", scatter_dimension=0, tiled=True)
    owned = lax.psum_scatter(owned_rows, "clus", scatter_dimension=1, tiled=True)
    cluster_ids = jnp.arange(clus_count)
    placed = (cluster_ids == clus_index).astype(jnp.float32)[:, None] * local_part[None, :]
    expansion_all = lax.psum(placed, ("clus", "lag"))
    eval_block = lax.dynamic_slice_in_dim(evaluation, clus_index * panel_block, panel_block, 1)
    far_block = jnp.dot(expansion_all, eval_block, precision=lax.Precision.HIGHEST)
    my_clusters = lax.dynamic_slice_in_dim(body_cluster, lag_index * body_block, body_block, 0)
    chooser = (my_clusters[:, None] == cluster_ids[None, :]).astype(jnp.float32)
    owned = owned + jnp.dot(chooser, far_block, precision=lax.Precision.HIGHEST)
    return owned.astype(jnp.bfloat16)


def solution(mesh):
    in_specs = (
        P(None, ("farm", "lag"), "clus"),
        P("lag", "clus", None),
        P(None, ("farm", "clus"), None),
        P("clus", None, "lag", None, None),
        P(),
        P(),
        P(),
        P(),
    )
    out_specs = P(("farm", "lag"), "clus")
    lags, clusters = mesh.shape["lag"], mesh.shape["clus"]
    if lags == 4 and clusters == 4:
        shards = functools.partial(shards_kernel, lags, clusters)
    else:
        shards = shards_general
    return jax.shard_map(shards, mesh=mesh, in_specs=in_specs, out_specs=out_specs, check_vma=False)
```

```python
import functools

import jax
import jax.numpy as jnp
from jax import lax
from jax.experimental import pallas as pl
from jax.experimental.pallas import tpu as pltpu
from jax.sharding import PartitionSpec as P

MESH = pl.DeviceIdType.MESH
F32 = jnp.float32
BF16 = jnp.bfloat16


GROUPS = ((0,), (1, 2), (3,))


def flipped(index, bits):
    low, high = lax.rem(index, 2), index // 2
    if bits & 1:
        low = 1 - low
    if bits & 2:
        high = 1 - high
    return high * 2 + low


def spread(tile, shape):
    column = jnp.concatenate([tile] * (shape[0] // 8), axis=0)
    return jnp.concatenate([column] * (shape[1] // 128), axis=1)


def encode(values, codes, scales):
    rows, columns = values.shape
    size = jnp.abs(values)
    peak = None
    for i in range(rows // 8):
        for j in range(columns // 128):
            part = size[8 * i : 8 * i + 8, 128 * j : 128 * j + 128]
            peak = part if peak is None else jnp.maximum(peak, part)
    peak = jnp.maximum(peak, 1e-33)
    scales[...] = peak * (1.0 / 32767.0)
    scaled = jnp.round(values * spread(32767.0 / peak, values.shape))
    codes[...] = scaled.astype(jnp.int32).astype(jnp.int16)


def decode(codes, scales):
    return codes[...].astype(jnp.int32).astype(F32) * spread(scales[...], codes.shape)


def body(
    lags, clusters,
    history, kernel, moments, coupling, evaluation, offsets_in, sources_in, cluster_in,
    out,
    offsets, pair_sources, body_cluster, moment_rows, hist, weights, mats, eval_block,
    rows, hist_send,
    core_send, core_recv, row_send, row_recv, row_scale, row_scaled, lag_send, lag_recv, lag_scale, lag_scaled, kept,
    moment_all, part_send, part_recv, local_all, far_rows, far,
    small_sem, hist_sem, weight_sem, mats_sem, eval_sem,
    hist_sems, core_sems, row_sems, lag_sems, row_scale_sems, lag_scale_sems, moment_sems, part_sems, local_sems,
):
    farm = lax.axis_index("farm")
    clus = lax.axis_index("clus")
    lag = lax.axis_index("lag")
    bodies, panels = out.shape
    lags_here = kernel.shape[0]
    pairs = coupling.shape[1]

    lag_peers = [(farm, clus, flipped(lag, j)) for j in range(lags)]
    clus_peers = [(farm, flipped(clus, r), lag) for r in range(clusters)]
    barrier = pltpu.get_barrier_semaphore()
    for peer in lag_peers[1:] + clus_peers[1:]:
        pl.semaphore_signal(barrier, inc=1, device_id=peer, device_id_type=MESH)

    small = [
        pltpu.make_async_copy(src, dst, small_sem.at[i])
        for i, (src, dst) in enumerate((
            (offsets_in, offsets), (sources_in, pair_sources),
            (cluster_in, body_cluster), (moments, moment_rows),
        ))
    ]
    small[0].start()
    hist_in = pltpu.make_async_copy(history, hist, hist_sem)
    hist_in.start()
    for copy in small[1:]:
        copy.start()
    blocks = [flipped(clus, 3), flipped(clus, 2), flipped(clus, 1), clus]
    weights_in = []
    for quad in range(clusters):
        columns = pl.ds(pl.multiple_of(blocks[quad] * panels, panels), panels)
        weights_in.append(
            pltpu.make_async_copy(
                kernel.at[:, :, columns], weights.at[quad], weight_sem.at[quad]
            )
        )
        weights_in[quad].start()
    mats_in = pltpu.make_async_copy(coupling.at[0], mats, mats_sem)
    mats_in.start()
    my_columns = pl.ds(pl.multiple_of(clus * panels, panels), panels)
    eval_in = pltpu.make_async_copy(evaluation.at[:, my_columns], eval_block, eval_sem)
    eval_in.start()

    small[0].wait()
    hist_in.wait()
    for l in range(lags_here):
        rows[l, 0:bodies] = hist[offsets[lag * lags_here + l]]
        for j in range(1, lags):
            hist_send[j - 1, l] = hist[offsets[lag_peers[j][2] * lags_here + l]]
    small[3].wait()
    moment_all[clus] = moment_rows[...].astype(F32)
    pl.semaphore_wait(barrier, lags - 1 + clusters - 1)

    sent = []

    def send(src, dst, sems, at, peer):
        copy = pltpu.make_async_remote_copy(
            src_ref=src, dst_ref=dst,
            send_sem=sems.at[(0,) + at], recv_sem=sems.at[(1,) + at],
            device_id=peer, device_id_type=MESH,
        )
        copy.start()
        sent.append(copy)
        return copy

    def send_history(j):
        landing = rows.at[:, pl.ds(j * bodies, bodies)]
        return send(hist_send.at[j - 1], landing, hist_sems, (j - 1,), lag_peers[j])

    hist_copies = {j: send_history(j) for j in (2, 1)}
    moment_copies = [
        send(moment_all.at[clus], moment_all.at[clus], moment_sems, (r - 1,), clus_peers[r])
        for r in range(1, clusters)
    ]

    group_copies, lag_copies = [[] for _ in GROUPS], {}

    def spans(group):
        return GROUPS[group][0] * bodies, len(GROUPS[group]) * bodies

    def product(group, quad):
        if group == 0:
            weights_in[quad].wait()
        top, height = spans(group)
        total = None
        for l in range(lags_here):
            term = jnp.dot(
                rows[l, top : top + height], weights[quad, l], preferred_element_type=F32
            )
            total = term if total is None else total + term
        return total

    def begin(group):
        for j in GROUPS[group]:
            if j > 0:
                hist_copies[j].wait_recv()
        part = pl.ds(0, spans(group)[1])
        for quad in range(clusters - 1):
            value, r = product(group, quad), clusters - 1 - quad
            if r == 1:
                core_send[group, part] = value
                group_copies[group].append(
                    send(
                        core_send.at[group, part], core_recv.at[group, part],
                        core_sems, (group,), clus_peers[1],
                    )
                )
            else:
                at = (group, r - 2)
                encode(value, row_send.at[at + (part,)], row_scale.at[at])
                group_copies[group] += [
                    send(
                        row_send.at[at + (part,)], row_recv.at[at + (part,)],
                        row_sems, at, clus_peers[r],
                    ),
                    send(row_scale.at[at], row_scaled.at[at], row_scale_sems, at, clus_peers[r]),
                ]
            if group == 0 and quad == 0:
                hist_copies[3] = send_history(3)
        kept[group, part] = product(group, clusters - 1)

    def finish(group):
        for copy in group_copies[group]:
            copy.wait_recv()
        part = pl.ds(0, spans(group)[1])
        total = kept[group, part] + core_recv[group, part]
        for i in range(2):
            total = total + decode(row_recv.at[group, i, part], row_scaled.at[group, i])
        if group == 0:
            kept[0, part] = total
        for at, j in enumerate(GROUPS[group]):
            if j > 0:
                i, top = j - 1, at * bodies
                encode(total[top : top + bodies], lag_send.at[i], lag_scale.at[i])
                lag_copies[j] = (
                    send(lag_send.at[i], lag_recv.at[i], lag_sems, (i,), lag_peers[j]),
                    send(lag_scale.at[i], lag_scaled.at[i], lag_scale_sems, (i,), lag_peers[j]),
                )

    begin(0)

    small[1].wait()
    mats_in.wait()
    for copy in moment_copies:
        copy.wait_recv()
    part = None
    for l in range(lags_here):
        slot = offsets[lag * lags_here + l]
        for k in range(pairs):
            row = moment_all[pair_sources[clus, k], pl.ds(slot, 1), :]
            row = jnp.broadcast_to(row, (16, row.shape[1])).astype(BF16)
            term = lax.dot_general(
                row, mats[k, l], (((1,), (1,)), ((), ())), preferred_element_type=F32
            )
            part = term if part is None else part + term
    part_send[...] = part[0:8]
    part_copies = [
        send(part_send, part_recv.at[j - 1], part_sems, (j - 1,), lag_peers[j])
        for j in range(1, lags)
    ]

    begin(1)
    finish(0)

    local = part_send[...]
    for j in range(1, lags):
        part_copies[j - 1].wait_recv()
        local = local + part_recv[j - 1]
    local_all[clus] = local
    local_copies = [
        send(local_all.at[clus], local_all.at[clus], local_sems, (r - 1,), clus_peers[r])
        for r in range(1, clusters)
    ]

    finish(1)
    begin(2)
    finish(2)

    small[2].wait()
    eval_in.wait()
    for copy in local_copies:
        copy.wait_recv()
    expansions = local_all[...].reshape(clusters * 8, local_all.shape[2])
    far_rows[...] = jnp.dot(
        expansions, eval_block[...], precision=lax.Precision.HIGHEST, preferred_element_type=F32
    )
    for b in range(bodies):
        far[b : b + 1, :] = far_rows[pl.ds(body_cluster[lag * bodies + b] * 8, 1), :]

    total = kept[0, 0:bodies]
    for j in range(1, lags):
        for copy in lag_copies[j]:
            copy.wait_recv()
        total = total + decode(lag_recv.at[j - 1], lag_scaled.at[j - 1])
    out[...] = (total + far[...]).astype(BF16)
    for copy in sent:
        copy.wait_send()


def shards_kernel(lags, clusters, history, kernel, moments, coupling, evaluation, offsets, pair_sources, body_cluster):
    slots, bodies, panels = history.shape
    lags_here, depth, _ = kernel.shape
    terms = moments.shape[2]
    moments = moments.reshape(slots, terms)
    pairs = coupling.shape[1]
    dma = pltpu.SemaphoreType.DMA
    anywhere = pl.BlockSpec(memory_space=pl.ANY)
    vmem = pl.BlockSpec(memory_space=pltpu.VMEM)
    block, double, groups = (bodies, panels), (2 * bodies, panels), len(GROUPS)
    flops = 2 * lags * bodies * lags_here * depth * clusters * panels
    return pl.pallas_call(
        functools.partial(body, lags, clusters),
        out_shape=pltpu.VMEM(block, BF16),
        in_specs=[anywhere] * 8,
        out_specs=vmem,
        scratch_shapes=[
            pltpu.SMEM(offsets.shape, jnp.int32),
            pltpu.SMEM(pair_sources.shape, jnp.int32),
            pltpu.SMEM(body_cluster.shape, jnp.int32),
            pltpu.VMEM((slots, terms), BF16),
            pltpu.VMEM((slots,) + block, BF16),
            pltpu.VMEM((clusters, lags_here, depth, panels), BF16),
            pltpu.VMEM((pairs, lags_here, terms, terms), BF16),
            pltpu.VMEM((terms, panels), F32),
            pltpu.VMEM((lags_here, lags * bodies, panels), BF16),
            pltpu.VMEM((lags - 1, lags_here) + block, BF16),
            pltpu.VMEM((groups,) + double, F32),
            pltpu.VMEM((groups,) + double, F32),
            pltpu.VMEM((groups, 2) + double, jnp.int16),
            pltpu.VMEM((groups, 2) + double, jnp.int16),
            pltpu.VMEM((groups, 2, 8, 128), F32),
            pltpu.VMEM((groups, 2, 8, 128), F32),
            pltpu.VMEM((lags - 1,) + block, jnp.int16),
            pltpu.VMEM((lags - 1,) + block, jnp.int16),
            pltpu.VMEM((lags - 1, 8, 128), F32),
            pltpu.VMEM((lags - 1, 8, 128), F32),
            pltpu.VMEM((groups,) + double, F32),
            pltpu.VMEM((clusters, slots, terms), F32),
            pltpu.VMEM((8, terms), F32),
            pltpu.VMEM((lags - 1, 8, terms), F32),
            pltpu.VMEM((clusters, 8, terms), F32),
            pltpu.VMEM((clusters * 8, panels), F32),
            pltpu.VMEM(block, F32),
            dma((4,)), dma, dma((clusters,)), dma, dma,
            dma((2, lags - 1)), dma((2, groups)), dma((2, groups, 2)), dma((2, lags - 1)),
            dma((2, groups, 2)), dma((2, lags - 1)),
            dma((2, clusters - 1)), dma((2, lags - 1)), dma((2, clusters - 1)),
        ],
        compiler_params=pltpu.CompilerParams(
            collective_id=0, has_side_effects=True, vmem_limit_bytes=63 * 1024 * 1024
        ),
        cost_estimate=pl.CostEstimate(
            flops=flops, bytes_accessed=2 * kernel.size, transcendentals=0
        ),
    )(history, kernel, moments, coupling, evaluation, offsets, pair_sources, body_cluster)


def shards_general(history, kernel, moments, coupling, evaluation, offsets, pair_sources, body_cluster):
    lag_index = lax.axis_index("lag")
    clus_index = lax.axis_index("clus")
    clus_count = lax.axis_size("clus")
    lags_here = kernel.shape[0]
    panel_block = history.shape[2]
    body_block = history.shape[1]
    picked = jnp.take(history, offsets, axis=0)
    arrived = lax.all_to_all(picked, "lag", split_axis=0, concat_axis=1, tiled=True)
    partial_value = jnp.einsum("lbp,lpq->bq", arrived, kernel, preferred_element_type=jnp.float32)
    my_lags = lag_index * lags_here + jnp.arange(lags_here)
    my_slots = jnp.take(offsets, my_lags, axis=0)
    wanted = jnp.take(moments, my_slots, axis=0)
    source_row = lax.dynamic_index_in_dim(pair_sources, clus_index, 0, keepdims=False)
    piece = lax.all_gather(wanted, "clus", axis=1, tiled=True)
    count = piece.shape[1]
    hits = (source_row[:, None] == jnp.arange(count)[None, :]).astype(jnp.float32)
    gathered = jnp.einsum("kn,lnm->klm", hits, piece.astype(jnp.float32))
    selected = gathered.astype(jnp.bfloat16)
    local_part = jnp.einsum(
        "klmn,kln->m", coupling[0], selected, preferred_element_type=jnp.float32
    )
    owned_rows = lax.psum_scatter(partial_value, "lag", scatter_dimension=0, tiled=True)
    owned = lax.psum_scatter(owned_rows, "clus", scatter_dimension=1, tiled=True)
    cluster_ids = jnp.arange(clus_count)
    placed = (cluster_ids == clus_index).astype(jnp.float32)[:, None] * local_part[None, :]
    expansion_all = lax.psum(placed, ("clus", "lag"))
    eval_block = lax.dynamic_slice_in_dim(evaluation, clus_index * panel_block, panel_block, 1)
    far_block = jnp.dot(expansion_all, eval_block, precision=lax.Precision.HIGHEST)
    my_clusters = lax.dynamic_slice_in_dim(body_cluster, lag_index * body_block, body_block, 0)
    chooser = (my_clusters[:, None] == cluster_ids[None, :]).astype(jnp.float32)
    owned = owned + jnp.dot(chooser, far_block, precision=lax.Precision.HIGHEST)
    return owned.astype(jnp.bfloat16)


def solution(mesh):
    in_specs = (
        P(None, ("farm", "lag"), "clus"),
        P("lag", "clus", None),
        P(None, ("farm", "clus"), None),
        P("clus", None, "lag", None, None),
        P(),
        P(),
        P(),
        P(),
    )
    out_specs = P(("farm", "lag"), "clus")
    lags, clusters = mesh.shape["lag"], mesh.shape["clus"]
    if lags == 4 and clusters == 4:
        shards = functools.partial(shards_kernel, lags, clusters)
    else:
        shards = shards_general
    return jax.shard_map(shards, mesh=mesh, in_specs=in_specs, out_specs=out_specs, check_vma=False)
```

```python
import functools

import jax
import jax.numpy as jnp
from jax import lax
from jax.experimental import pallas as pl
from jax.experimental.pallas import tpu as pltpu
from jax.sharding import PartitionSpec as P

MESH = pl.DeviceIdType.MESH
F32 = jnp.float32
BF16 = jnp.bfloat16


GROUPS = ((0,), (1, 2), (3,))
LAG_ORDER = (0, 1, 3, 2)


def flipped(index, bits):
    low, high = lax.rem(index, 2), index // 2
    if bits & 1:
        low = 1 - low
    if bits & 2:
        high = 1 - high
    return high * 2 + low


def spread(tile, shape):
    column = jnp.concatenate([tile] * (shape[0] // 8), axis=0)
    return jnp.concatenate([column] * (shape[1] // 128), axis=1)


def encode(values, codes, scales):
    rows, columns = values.shape
    size = jnp.abs(values)
    peak = None
    for i in range(rows // 8):
        for j in range(columns // 128):
            part = size[8 * i : 8 * i + 8, 128 * j : 128 * j + 128]
            peak = part if peak is None else jnp.maximum(peak, part)
    peak = jnp.maximum(peak, 1e-33)
    scales[...] = peak * (1.0 / 32767.0)
    scaled = jnp.round(values * spread(32767.0 / peak, values.shape))
    codes[...] = scaled.astype(jnp.int32).astype(jnp.int16)


def decode(codes, scales):
    return codes[...].astype(jnp.int32).astype(F32) * spread(scales[...], codes.shape)


def body(
    lags, clusters,
    history, kernel, moments, coupling, evaluation, offsets_in, sources_in, cluster_in,
    out,
    offsets, pair_sources, body_cluster, moment_rows, hist, weights, mats, eval_block,
    rows, hist_send,
    core_send, core_recv, row_send, row_recv, row_scale, row_scaled, lag_send, lag_recv, lag_scale, lag_scaled, kept,
    moment_all, part_send, part_recv, local_all, far_rows, far,
    small_sem, hist_sem, weight_sem, mats_sem, eval_sem,
    hist_sems, core_sems, row_sems, lag_sems, row_scale_sems, lag_scale_sems, moment_sems, part_sems, local_sems,
):
    farm = lax.axis_index("farm")
    clus = lax.axis_index("clus")
    lag = lax.axis_index("lag")
    bodies, panels = out.shape
    lags_here = kernel.shape[0]
    pairs = coupling.shape[1]

    lag_peers = [(farm, clus, flipped(lag, bits)) for bits in LAG_ORDER]
    clus_peers = [(farm, flipped(clus, r), lag) for r in range(clusters)]
    barrier = pltpu.get_barrier_semaphore()
    for peer in lag_peers[1:] + clus_peers[1:]:
        pl.semaphore_signal(barrier, inc=1, device_id=peer, device_id_type=MESH)

    small = [
        pltpu.make_async_copy(src, dst, small_sem.at[i])
        for i, (src, dst) in enumerate((
            (offsets_in, offsets), (sources_in, pair_sources),
            (cluster_in, body_cluster), (moments, moment_rows),
        ))
    ]
    small[0].start()
    hist_in = pltpu.make_async_copy(history, hist, hist_sem)
    hist_in.start()
    for copy in small[1:]:
        copy.start()
    blocks = [flipped(clus, 3), flipped(clus, 2), flipped(clus, 1), clus]
    weights_in = []
    for quad in range(clusters):
        columns = pl.ds(pl.multiple_of(blocks[quad] * panels, panels), panels)
        weights_in.append(
            pltpu.make_async_copy(
                kernel.at[:, :, columns], weights.at[quad], weight_sem.at[quad]
            )
        )
        weights_in[quad].start()
    mats_in = pltpu.make_async_copy(coupling.at[0], mats, mats_sem)
    mats_in.start()
    my_columns = pl.ds(pl.multiple_of(clus * panels, panels), panels)
    eval_in = pltpu.make_async_copy(evaluation.at[:, my_columns], eval_block, eval_sem)
    eval_in.start()

    small[0].wait()
    hist_in.wait()
    for l in range(lags_here):
        rows[l, 0:bodies] = hist[offsets[lag * lags_here + l]]
        for j in range(1, lags):
            hist_send[j - 1, l] = hist[offsets[lag_peers[j][2] * lags_here + l]]
    small[3].wait()
    moment_all[clus] = moment_rows[...].astype(F32)
    pl.semaphore_wait(barrier, lags - 1 + clusters - 1)

    sent = []

    def send(src, dst, sems, at, peer):
        copy = pltpu.make_async_remote_copy(
            src_ref=src, dst_ref=dst,
            send_sem=sems.at[(0,) + at], recv_sem=sems.at[(1,) + at],
            device_id=peer, device_id_type=MESH,
        )
        copy.start()
        sent.append(copy)
        return copy

    def send_history(j):
        landing = rows.at[:, pl.ds(j * bodies, bodies)]
        return send(hist_send.at[j - 1], landing, hist_sems, (j - 1,), lag_peers[j])

    hist_copies = {j: send_history(j) for j in (2, 1)}
    moment_copies = [
        send(moment_all.at[clus], moment_all.at[clus], moment_sems, (r - 1,), clus_peers[r])
        for r in range(1, clusters)
    ]

    group_copies, lag_copies = [[] for _ in GROUPS], {}

    def spans(group):
        return GROUPS[group][0] * bodies, len(GROUPS[group]) * bodies

    def product(group, quad):
        if group == 0:
            weights_in[quad].wait()
        top, height = spans(group)
        total = None
        for l in range(lags_here):
            term = jnp.dot(
                rows[l, top : top + height], weights[quad, l], preferred_element_type=F32
            )
            total = term if total is None else total + term
        return total

    def begin(group):
        for j in GROUPS[group]:
            if j > 0:
                hist_copies[j].wait_recv()
        part = pl.ds(0, spans(group)[1])
        for quad in range(clusters - 1):
            value, r = product(group, quad), clusters - 1 - quad
            if r == 1:
                core_send[group, part] = value
                group_copies[group].append(
                    send(
                        core_send.at[group, part], core_recv.at[group, part],
                        core_sems, (group,), clus_peers[1],
                    )
                )
            else:
                at = (group, r - 2)
                encode(value, row_send.at[at + (part,)], row_scale.at[at])
                group_copies[group] += [
                    send(
                        row_send.at[at + (part,)], row_recv.at[at + (part,)],
                        row_sems, at, clus_peers[r],
                    ),
                    send(row_scale.at[at], row_scaled.at[at], row_scale_sems, at, clus_peers[r]),
                ]
            if group == 0 and quad == 0:
                hist_copies[3] = send_history(3)
        kept[group, part] = product(group, clusters - 1)

    def finish(group):
        for copy in group_copies[group]:
            copy.wait_recv()
        part = pl.ds(0, spans(group)[1])
        total = kept[group, part] + core_recv[group, part]
        for i in range(2):
            total = total + decode(row_recv.at[group, i, part], row_scaled.at[group, i])
        if group == 0:
            kept[0, part] = total
        for at, j in enumerate(GROUPS[group]):
            if j > 0:
                i, top = j - 1, at * bodies
                encode(total[top : top + bodies], lag_send.at[i], lag_scale.at[i])
                lag_copies[j] = (
                    send(lag_send.at[i], lag_recv.at[i], lag_sems, (i,), lag_peers[j]),
                    send(lag_scale.at[i], lag_scaled.at[i], lag_scale_sems, (i,), lag_peers[j]),
                )

    begin(0)

    small[1].wait()
    mats_in.wait()
    for copy in moment_copies:
        copy.wait_recv()
    part = None
    for l in range(lags_here):
        slot = offsets[lag * lags_here + l]
        for k in range(pairs):
            row = moment_all[pair_sources[clus, k], pl.ds(slot, 1), :]
            row = jnp.broadcast_to(row, (16, row.shape[1])).astype(BF16)
            term = lax.dot_general(
                row, mats[k, l], (((1,), (1,)), ((), ())), preferred_element_type=F32
            )
            part = term if part is None else part + term
    part_send[...] = part[0:8]
    part_copies = [
        send(part_send, part_recv.at[j - 1], part_sems, (j - 1,), lag_peers[j])
        for j in range(1, lags)
    ]

    begin(1)
    finish(0)

    local = part_send[...]
    for j in range(1, lags):
        part_copies[j - 1].wait_recv()
        local = local + part_recv[j - 1]
    local_all[clus] = local
    local_copies = [
        send(local_all.at[clus], local_all.at[clus], local_sems, (r - 1,), clus_peers[r])
        for r in range(1, clusters)
    ]

    begin(2)
    finish(1)
    finish(2)

    small[2].wait()
    eval_in.wait()
    for copy in local_copies:
        copy.wait_recv()
    expansions = local_all[...].reshape(clusters * 8, local_all.shape[2])
    far_rows[...] = jnp.dot(
        expansions, eval_block[...], precision=lax.Precision.HIGHEST, preferred_element_type=F32
    )
    for b in range(bodies):
        far[b : b + 1, :] = far_rows[pl.ds(body_cluster[lag * bodies + b] * 8, 1), :]

    total = kept[0, 0:bodies]
    for j in range(1, lags):
        for copy in lag_copies[j]:
            copy.wait_recv()
        total = total + decode(lag_recv.at[j - 1], lag_scaled.at[j - 1])
    out[...] = (total + far[...]).astype(BF16)
    for copy in sent:
        copy.wait_send()


def shards_kernel(lags, clusters, history, kernel, moments, coupling, evaluation, offsets, pair_sources, body_cluster):
    slots, bodies, panels = history.shape
    lags_here, depth, _ = kernel.shape
    terms = moments.shape[2]
    moments = moments.reshape(slots, terms)
    pairs = coupling.shape[1]
    dma = pltpu.SemaphoreType.DMA
    anywhere = pl.BlockSpec(memory_space=pl.ANY)
    vmem = pl.BlockSpec(memory_space=pltpu.VMEM)
    block, double, groups = (bodies, panels), (2 * bodies, panels), len(GROUPS)
    flops = 2 * lags * bodies * lags_here * depth * clusters * panels
    return pl.pallas_call(
        functools.partial(body, lags, clusters),
        out_shape=pltpu.VMEM(block, BF16),
        in_specs=[anywhere] * 8,
        out_specs=vmem,
        scratch_shapes=[
            pltpu.SMEM(offsets.shape, jnp.int32),
            pltpu.SMEM(pair_sources.shape, jnp.int32),
            pltpu.SMEM(body_cluster.shape, jnp.int32),
            pltpu.VMEM((slots, terms), BF16),
            pltpu.VMEM((slots,) + block, BF16),
            pltpu.VMEM((clusters, lags_here, depth, panels), BF16),
            pltpu.VMEM((pairs, lags_here, terms, terms), BF16),
            pltpu.VMEM((terms, panels), F32),
            pltpu.VMEM((lags_here, lags * bodies, panels), BF16),
            pltpu.VMEM((lags - 1, lags_here) + block, BF16),
            pltpu.VMEM((groups,) + double, F32),
            pltpu.VMEM((groups,) + double, F32),
            pltpu.VMEM((groups, 2) + double, jnp.int16),
            pltpu.VMEM((groups, 2) + double, jnp.int16),
            pltpu.VMEM((groups, 2, 8, 128), F32),
            pltpu.VMEM((groups, 2, 8, 128), F32),
            pltpu.VMEM((lags - 1,) + block, jnp.int16),
            pltpu.VMEM((lags - 1,) + block, jnp.int16),
            pltpu.VMEM((lags - 1, 8, 128), F32),
            pltpu.VMEM((lags - 1, 8, 128), F32),
            pltpu.VMEM((groups,) + double, F32),
            pltpu.VMEM((clusters, slots, terms), F32),
            pltpu.VMEM((8, terms), F32),
            pltpu.VMEM((lags - 1, 8, terms), F32),
            pltpu.VMEM((clusters, 8, terms), F32),
            pltpu.VMEM((clusters * 8, panels), F32),
            pltpu.VMEM(block, F32),
            dma((4,)), dma, dma((clusters,)), dma, dma,
            dma((2, lags - 1)), dma((2, groups)), dma((2, groups, 2)), dma((2, lags - 1)),
            dma((2, groups, 2)), dma((2, lags - 1)),
            dma((2, clusters - 1)), dma((2, lags - 1)), dma((2, clusters - 1)),
        ],
        compiler_params=pltpu.CompilerParams(
            collective_id=0, has_side_effects=True, vmem_limit_bytes=63 * 1024 * 1024
        ),
        cost_estimate=pl.CostEstimate(
            flops=flops, bytes_accessed=2 * kernel.size, transcendentals=0
        ),
    )(history, kernel, moments, coupling, evaluation, offsets, pair_sources, body_cluster)


def shards_general(history, kernel, moments, coupling, evaluation, offsets, pair_sources, body_cluster):
    lag_index = lax.axis_index("lag")
    clus_index = lax.axis_index("clus")
    clus_count = lax.axis_size("clus")
    lags_here = kernel.shape[0]
    panel_block = history.shape[2]
    body_block = history.shape[1]
    picked = jnp.take(history, offsets, axis=0)
    arrived = lax.all_to_all(picked, "lag", split_axis=0, concat_axis=1, tiled=True)
    partial_value = jnp.einsum("lbp,lpq->bq", arrived, kernel, preferred_element_type=jnp.float32)
    my_lags = lag_index * lags_here + jnp.arange(lags_here)
    my_slots = jnp.take(offsets, my_lags, axis=0)
    wanted = jnp.take(moments, my_slots, axis=0)
    source_row = lax.dynamic_index_in_dim(pair_sources, clus_index, 0, keepdims=False)
    piece = lax.all_gather(wanted, "clus", axis=1, tiled=True)
    count = piece.shape[1]
    hits = (source_row[:, None] == jnp.arange(count)[None, :]).astype(jnp.float32)
    gathered = jnp.einsum("kn,lnm->klm", hits, piece.astype(jnp.float32))
    selected = gathered.astype(jnp.bfloat16)
    local_part = jnp.einsum(
        "klmn,kln->m", coupling[0], selected, preferred_element_type=jnp.float32
    )
    owned_rows = lax.psum_scatter(partial_value, "lag", scatter_dimension=0, tiled=True)
    owned = lax.psum_scatter(owned_rows, "clus", scatter_dimension=1, tiled=True)
    cluster_ids = jnp.arange(clus_count)
    placed = (cluster_ids == clus_index).astype(jnp.float32)[:, None] * local_part[None, :]
    expansion_all = lax.psum(placed, ("clus", "lag"))
    eval_block = lax.dynamic_slice_in_dim(evaluation, clus_index * panel_block, panel_block, 1)
    far_block = jnp.dot(expansion_all, eval_block, precision=lax.Precision.HIGHEST)
    my_clusters = lax.dynamic_slice_in_dim(body_cluster, lag_index * body_block, body_block, 0)
    chooser = (my_clusters[:, None] == cluster_ids[None, :]).astype(jnp.float32)
    owned = owned + jnp.dot(chooser, far_block, precision=lax.Precision.HIGHEST)
    return owned.astype(jnp.bfloat16)


def solution(mesh):
    in_specs = (
        P(None, ("farm", "lag"), "clus"),
        P("lag", "clus", None),
        P(None, ("farm", "clus"), None),
        P("clus", None, "lag", None, None),
        P(),
        P(),
        P(),
        P(),
    )
    out_specs = P(("farm", "lag"), "clus")
    lags, clusters = mesh.shape["lag"], mesh.shape["clus"]
    if lags == 4 and clusters == 4:
        shards = functools.partial(shards_kernel, lags, clusters)
    else:
        shards = shards_general
    return jax.shard_map(shards, mesh=mesh, in_specs=in_specs, out_specs=out_specs, check_vma=False)
```

```python
import functools

import jax
import jax.numpy as jnp
from jax import lax
from jax.experimental import pallas as pl
from jax.experimental.pallas import tpu as pltpu
from jax.sharding import PartitionSpec as P

MESH = pl.DeviceIdType.MESH
F32 = jnp.float32
BF16 = jnp.bfloat16


GROUPS = ((0,), (1, 2), (3,))
LAG_ORDER = (0, 1, 3, 2)


def flipped(index, bits):
    low, high = lax.rem(index, 2), index // 2
    if bits & 1:
        low = 1 - low
    if bits & 2:
        high = 1 - high
    return high * 2 + low


def spread(tile, shape):
    column = jnp.concatenate([tile] * (shape[0] // 8), axis=0)
    return jnp.concatenate([column] * (shape[1] // 128), axis=1)


def encode(values, codes, scales):
    rows, columns = values.shape
    size = jnp.abs(values)
    peak = None
    for i in range(rows // 8):
        for j in range(columns // 128):
            part = size[8 * i : 8 * i + 8, 128 * j : 128 * j + 128]
            peak = part if peak is None else jnp.maximum(peak, part)
    peak = jnp.maximum(peak, 1e-33)
    scales[...] = peak * (1.0 / 32767.0)
    scaled = jnp.round(values * spread(32767.0 / peak, values.shape))
    codes[...] = scaled.astype(jnp.int32).astype(jnp.int16)


def decode(codes, scales):
    return codes[...].astype(jnp.int32).astype(F32) * spread(scales[...], codes.shape)


def body(
    lags, clusters,
    history, kernel, moments, coupling, evaluation, offsets_in, sources_in, cluster_in,
    out,
    offsets, pair_sources, body_cluster, moment_rows, hist, weights, mats, eval_block,
    rows, hist_send,
    core_send, core_recv, row_send, row_recv, row_scale, row_scaled, lag_send, lag_recv, lag_scale, lag_scaled, kept, early,
    moment_all, part_send, part_recv, local_all, far_rows, far,
    small_sem, hist_sem, weight_sem, mats_sem, eval_sem,
    hist_sems, core_sems, row_sems, lag_sems, row_scale_sems, lag_scale_sems, moment_sems, part_sems, local_sems,
):
    farm = lax.axis_index("farm")
    clus = lax.axis_index("clus")
    lag = lax.axis_index("lag")
    bodies, panels = out.shape
    lags_here = kernel.shape[0]
    pairs = coupling.shape[1]

    lag_peers = [(farm, clus, flipped(lag, bits)) for bits in LAG_ORDER]
    clus_peers = [(farm, flipped(clus, r), lag) for r in range(clusters)]
    barrier = pltpu.get_barrier_semaphore()
    for peer in lag_peers[1:] + clus_peers[1:]:
        pl.semaphore_signal(barrier, inc=1, device_id=peer, device_id_type=MESH)

    small = [
        pltpu.make_async_copy(src, dst, small_sem.at[i])
        for i, (src, dst) in enumerate((
            (offsets_in, offsets), (sources_in, pair_sources),
            (cluster_in, body_cluster), (moments, moment_rows),
        ))
    ]
    small[0].start()
    hist_in = pltpu.make_async_copy(history, hist, hist_sem)
    hist_in.start()
    for copy in small[1:]:
        copy.start()
    blocks = [flipped(clus, 3), flipped(clus, 2), flipped(clus, 1), clus]
    weights_in = []
    for quad in range(clusters):
        columns = pl.ds(pl.multiple_of(blocks[quad] * panels, panels), panels)
        weights_in.append(
            pltpu.make_async_copy(
                kernel.at[:, :, columns], weights.at[quad], weight_sem.at[quad]
            )
        )
        weights_in[quad].start()
    mats_in = pltpu.make_async_copy(coupling.at[0], mats, mats_sem)
    mats_in.start()
    my_columns = pl.ds(pl.multiple_of(clus * panels, panels), panels)
    eval_in = pltpu.make_async_copy(evaluation.at[:, my_columns], eval_block, eval_sem)
    eval_in.start()

    small[0].wait()
    hist_in.wait()
    for l in range(lags_here):
        rows[l, 0:bodies] = hist[offsets[lag * lags_here + l]]
        for j in range(1, lags):
            hist_send[j - 1, l] = hist[offsets[lag_peers[j][2] * lags_here + l]]
    small[3].wait()
    moment_all[clus] = moment_rows[...].astype(F32)
    pl.semaphore_wait(barrier, lags - 1 + clusters - 1)

    sent = []

    def send(src, dst, sems, at, peer):
        copy = pltpu.make_async_remote_copy(
            src_ref=src, dst_ref=dst,
            send_sem=sems.at[(0,) + at], recv_sem=sems.at[(1,) + at],
            device_id=peer, device_id_type=MESH,
        )
        copy.start()
        sent.append(copy)
        return copy

    def send_history(j):
        return [
            send(
                hist_send.at[j - 1, l], rows.at[l, pl.ds(j * bodies, bodies)],
                hist_sems, (j - 1, l), lag_peers[j],
            )
            for l in range(lags_here)
        ]

    hist_copies = {j: send_history(j) for j in (2, 1)}
    moment_copies = [
        send(moment_all.at[clus], moment_all.at[clus], moment_sems, (r - 1,), clus_peers[r])
        for r in range(1, clusters)
    ]

    group_copies, lag_copies = [[] for _ in GROUPS], {}

    last = len(GROUPS) - 1

    def spans(group):
        return GROUPS[group][0] * bodies, len(GROUPS[group]) * bodies

    def product(group, quad):
        if group == 0:
            weights_in[quad].wait()
        top, height = spans(group)
        total = early[quad] if group == last else None
        for l in range(lags_here - 1 if group == last else 0, lags_here):
            term = jnp.dot(
                rows[l, top : top + height], weights[quad, l], preferred_element_type=F32
            )
            total = term if total is None else total + term
        return total

    def begin(group):
        arriving = [hist_copies[j] for j in GROUPS[group] if j > 0]
        for l in range(lags_here):
            for copies in arriving:
                copies[l].wait_recv()
            if group == last and l < lags_here - 1:
                top, height = spans(group)
                for quad in range(clusters):
                    term = jnp.dot(
                        rows[l, top : top + height], weights[quad, l], preferred_element_type=F32
                    )
                    early[quad] = term if l == 0 else early[quad] + term
        part = pl.ds(0, spans(group)[1])
        for quad in range(clusters - 1):
            value, r = product(group, quad), clusters - 1 - quad
            if r == 1:
                core_send[group, part] = value
                group_copies[group].append(
                    send(
                        core_send.at[group, part], core_recv.at[group, part],
                        core_sems, (group,), clus_peers[1],
                    )
                )
            else:
                at = (group, r - 2)
                encode(value, row_send.at[at + (part,)], row_scale.at[at])
                group_copies[group] += [
                    send(
                        row_send.at[at + (part,)], row_recv.at[at + (part,)],
                        row_sems, at, clus_peers[r],
                    ),
                    send(row_scale.at[at], row_scaled.at[at], row_scale_sems, at, clus_peers[r]),
                ]
            if group == 0 and quad == 0:
                hist_copies[3] = send_history(3)
        kept[group, part] = product(group, clusters - 1)

    def finish(group):
        for copy in group_copies[group]:
            copy.wait_recv()
        part = pl.ds(0, spans(group)[1])
        total = kept[group, part] + core_recv[group, part]
        for i in range(2):
            total = total + decode(row_recv.at[group, i, part], row_scaled.at[group, i])
        if group == 0:
            kept[0, part] = total
        for at, j in enumerate(GROUPS[group]):
            if j > 0:
                i, top = j - 1, at * bodies
                encode(total[top : top + bodies], lag_send.at[i], lag_scale.at[i])
                lag_copies[j] = (
                    send(lag_send.at[i], lag_recv.at[i], lag_sems, (i,), lag_peers[j]),
                    send(lag_scale.at[i], lag_scaled.at[i], lag_scale_sems, (i,), lag_peers[j]),
                )

    begin(0)

    small[1].wait()
    mats_in.wait()
    for copy in moment_copies:
        copy.wait_recv()
    part = None
    for l in range(lags_here):
        slot = offsets[lag * lags_here + l]
        for k in range(pairs):
            row = moment_all[pair_sources[clus, k], pl.ds(slot, 1), :]
            row = jnp.broadcast_to(row, (16, row.shape[1])).astype(BF16)
            term = lax.dot_general(
                row, mats[k, l], (((1,), (1,)), ((), ())), preferred_element_type=F32
            )
            part = term if part is None else part + term
    part_send[...] = part[0:8]
    part_copies = [
        send(part_send, part_recv.at[j - 1], part_sems, (j - 1,), lag_peers[j])
        for j in range(1, lags)
    ]

    begin(1)
    finish(0)

    local = part_send[...]
    for j in range(1, lags):
        part_copies[j - 1].wait_recv()
        local = local + part_recv[j - 1]
    local_all[clus] = local
    local_copies = [
        send(local_all.at[clus], local_all.at[clus], local_sems, (r - 1,), clus_peers[r])
        for r in range(1, clusters)
    ]

    begin(2)
    finish(1)
    finish(2)

    small[2].wait()
    eval_in.wait()
    for copy in local_copies:
        copy.wait_recv()
    expansions = local_all[...].reshape(clusters * 8, local_all.shape[2])
    far_rows[...] = jnp.dot(
        expansions, eval_block[...], precision=lax.Precision.HIGHEST, preferred_element_type=F32
    )
    for b in range(bodies):
        far[b : b + 1, :] = far_rows[pl.ds(body_cluster[lag * bodies + b] * 8, 1), :]

    total = kept[0, 0:bodies]
    for j in range(1, lags):
        for copy in lag_copies[j]:
            copy.wait_recv()
        total = total + decode(lag_recv.at[j - 1], lag_scaled.at[j - 1])
    out[...] = (total + far[...]).astype(BF16)
    for copy in sent:
        copy.wait_send()


def shards_kernel(lags, clusters, history, kernel, moments, coupling, evaluation, offsets, pair_sources, body_cluster):
    slots, bodies, panels = history.shape
    lags_here, depth, _ = kernel.shape
    terms = moments.shape[2]
    moments = moments.reshape(slots, terms)
    pairs = coupling.shape[1]
    dma = pltpu.SemaphoreType.DMA
    anywhere = pl.BlockSpec(memory_space=pl.ANY)
    vmem = pl.BlockSpec(memory_space=pltpu.VMEM)
    block, double, groups = (bodies, panels), (2 * bodies, panels), len(GROUPS)
    flops = 2 * lags * bodies * lags_here * depth * clusters * panels
    return pl.pallas_call(
        functools.partial(body, lags, clusters),
        out_shape=pltpu.VMEM(block, BF16),
        in_specs=[anywhere] * 8,
        out_specs=vmem,
        scratch_shapes=[
            pltpu.SMEM(offsets.shape, jnp.int32),
            pltpu.SMEM(pair_sources.shape, jnp.int32),
            pltpu.SMEM(body_cluster.shape, jnp.int32),
            pltpu.VMEM((slots, terms), BF16),
            pltpu.VMEM((slots,) + block, BF16),
            pltpu.VMEM((clusters, lags_here, depth, panels), BF16),
            pltpu.VMEM((pairs, lags_here, terms, terms), BF16),
            pltpu.VMEM((terms, panels), F32),
            pltpu.VMEM((lags_here, lags * bodies, panels), BF16),
            pltpu.VMEM((lags - 1, lags_here) + block, BF16),
            pltpu.VMEM((groups,) + double, F32),
            pltpu.VMEM((groups,) + double, F32),
            pltpu.VMEM((groups, 2) + double, jnp.int16),
            pltpu.VMEM((groups, 2) + double, jnp.int16),
            pltpu.VMEM((groups, 2, 8, 128), F32),
            pltpu.VMEM((groups, 2, 8, 128), F32),
            pltpu.VMEM((lags - 1,) + block, jnp.int16),
            pltpu.VMEM((lags - 1,) + block, jnp.int16),
            pltpu.VMEM((lags - 1, 8, 128), F32),
            pltpu.VMEM((lags - 1, 8, 128), F32),
            pltpu.VMEM((groups,) + double, F32),
            pltpu.VMEM((clusters,) + block, F32),
            pltpu.VMEM((clusters, slots, terms), F32),
            pltpu.VMEM((8, terms), F32),
            pltpu.VMEM((lags - 1, 8, terms), F32),
            pltpu.VMEM((clusters, 8, terms), F32),
            pltpu.VMEM((clusters * 8, panels), F32),
            pltpu.VMEM(block, F32),
            dma((4,)), dma, dma((clusters,)), dma, dma,
            dma((2, lags - 1, lags_here)), dma((2, groups)), dma((2, groups, 2)), dma((2, lags - 1)),
            dma((2, groups, 2)), dma((2, lags - 1)),
            dma((2, clusters - 1)), dma((2, lags - 1)), dma((2, clusters - 1)),
        ],
        compiler_params=pltpu.CompilerParams(
            collective_id=0, has_side_effects=True, vmem_limit_bytes=63 * 1024 * 1024
        ),
        cost_estimate=pl.CostEstimate(
            flops=flops, bytes_accessed=2 * kernel.size, transcendentals=0
        ),
    )(history, kernel, moments, coupling, evaluation, offsets, pair_sources, body_cluster)


def shards_general(history, kernel, moments, coupling, evaluation, offsets, pair_sources, body_cluster):
    lag_index = lax.axis_index("lag")
    clus_index = lax.axis_index("clus")
    clus_count = lax.axis_size("clus")
    lags_here = kernel.shape[0]
    panel_block = history.shape[2]
    body_block = history.shape[1]
    picked = jnp.take(history, offsets, axis=0)
    arrived = lax.all_to_all(picked, "lag", split_axis=0, concat_axis=1, tiled=True)
    partial_value = jnp.einsum("lbp,lpq->bq", arrived, kernel, preferred_element_type=jnp.float32)
    my_lags = lag_index * lags_here + jnp.arange(lags_here)
    my_slots = jnp.take(offsets, my_lags, axis=0)
    wanted = jnp.take(moments, my_slots, axis=0)
    source_row = lax.dynamic_index_in_dim(pair_sources, clus_index, 0, keepdims=False)
    piece = lax.all_gather(wanted, "clus", axis=1, tiled=True)
    count = piece.shape[1]
    hits = (source_row[:, None] == jnp.arange(count)[None, :]).astype(jnp.float32)
    gathered = jnp.einsum("kn,lnm->klm", hits, piece.astype(jnp.float32))
    selected = gathered.astype(jnp.bfloat16)
    local_part = jnp.einsum(
        "klmn,kln->m", coupling[0], selected, preferred_element_type=jnp.float32
    )
    owned_rows = lax.psum_scatter(partial_value, "lag", scatter_dimension=0, tiled=True)
    owned = lax.psum_scatter(owned_rows, "clus", scatter_dimension=1, tiled=True)
    cluster_ids = jnp.arange(clus_count)
    placed = (cluster_ids == clus_index).astype(jnp.float32)[:, None] * local_part[None, :]
    expansion_all = lax.psum(placed, ("clus", "lag"))
    eval_block = lax.dynamic_slice_in_dim(evaluation, clus_index * panel_block, panel_block, 1)
    far_block = jnp.dot(expansion_all, eval_block, precision=lax.Precision.HIGHEST)
    my_clusters = lax.dynamic_slice_in_dim(body_cluster, lag_index * body_block, body_block, 0)
    chooser = (my_clusters[:, None] == cluster_ids[None, :]).astype(jnp.float32)
    owned = owned + jnp.dot(chooser, far_block, precision=lax.Precision.HIGHEST)
    return owned.astype(jnp.bfloat16)


def solution(mesh):
    in_specs = (
        P(None, ("farm", "lag"), "clus"),
        P("lag", "clus", None),
        P(None, ("farm", "clus"), None),
        P("clus", None, "lag", None, None),
        P(),
        P(),
        P(),
        P(),
    )
    out_specs = P(("farm", "lag"), "clus")
    lags, clusters = mesh.shape["lag"], mesh.shape["clus"]
    if lags == 4 and clusters == 4:
        shards = functools.partial(shards_kernel, lags, clusters)
    else:
        shards = shards_general
    return jax.shard_map(shards, mesh=mesh, in_specs=in_specs, out_specs=out_specs, check_vma=False)
```

```python
import functools

import jax
import jax.numpy as jnp
from jax import lax
from jax.experimental import pallas as pl
from jax.experimental.pallas import tpu as pltpu
from jax.sharding import PartitionSpec as P

MESH = pl.DeviceIdType.MESH
F32 = jnp.float32
BF16 = jnp.bfloat16


GROUPS = ((0,), (1, 2), (3,))
LAG_ORDER = (0, 1, 3, 2)


def flipped(index, bits):
    low, high = lax.rem(index, 2), index // 2
    if bits & 1:
        low = 1 - low
    if bits & 2:
        high = 1 - high
    return high * 2 + low


def spread(tile, shape):
    column = jnp.concatenate([tile] * (shape[0] // 8), axis=0)
    return jnp.concatenate([column] * (shape[1] // 128), axis=1)


def encode(values, codes, scales):
    rows, columns = values.shape
    size = jnp.abs(values)
    peak = None
    for i in range(rows // 8):
        for j in range(columns // 128):
            part = size[8 * i : 8 * i + 8, 128 * j : 128 * j + 128]
            peak = part if peak is None else jnp.maximum(peak, part)
    peak = jnp.maximum(peak, 1e-33)
    scales[...] = peak * (1.0 / 32767.0)
    scaled = jnp.round(values * spread(32767.0 / peak, values.shape))
    codes[...] = scaled.astype(jnp.int32).astype(jnp.int16)


def decode(codes, scales):
    return codes[...].astype(jnp.int32).astype(F32) * spread(scales[...], codes.shape)


def body(
    lags, clusters,
    history, kernel, moments, coupling, evaluation, offsets_in, sources_in, cluster_in,
    out,
    offsets, pair_sources, body_cluster, moment_rows, hist, weights, mats, eval_block,
    rows, hist_send,
    core_send, core_recv, row_send, row_recv, row_scale, row_scaled, lag_send, lag_recv, lag_scale, lag_scaled, kept,
    moment_all, part_send, part_recv, local_all, far_rows, far,
    small_sem, hist_sem, weight_sem, mats_sem, eval_sem,
    hist_sems, core_sems, row_sems, lag_sems, row_scale_sems, lag_scale_sems, moment_sems, part_sems, local_sems,
):
    farm = lax.axis_index("farm")
    clus = lax.axis_index("clus")
    lag = lax.axis_index("lag")
    bodies, panels = out.shape
    lags_here = kernel.shape[0]
    pairs = coupling.shape[1]

    lag_peers = [(farm, clus, flipped(lag, bits)) for bits in LAG_ORDER]
    clus_peers = [(farm, flipped(clus, r), lag) for r in range(clusters)]
    barrier = pltpu.get_barrier_semaphore()
    for peer in lag_peers[1:] + clus_peers[1:]:
        pl.semaphore_signal(barrier, inc=1, device_id=peer, device_id_type=MESH)

    small = [
        pltpu.make_async_copy(src, dst, small_sem.at[i])
        for i, (src, dst) in enumerate((
            (offsets_in, offsets), (sources_in, pair_sources),
            (cluster_in, body_cluster), (moments, moment_rows),
        ))
    ]
    small[0].start()
    hist_in = pltpu.make_async_copy(history, hist, hist_sem)
    hist_in.start()
    for copy in small[1:]:
        copy.start()
    blocks = [flipped(clus, 3), flipped(clus, 2), flipped(clus, 1), clus]
    weights_in = []
    for quad in range(clusters):
        columns = pl.ds(pl.multiple_of(blocks[quad] * panels, panels), panels)
        weights_in.append(
            pltpu.make_async_copy(
                kernel.at[:, :, columns], weights.at[quad], weight_sem.at[quad]
            )
        )
        weights_in[quad].start()
    mats_in = pltpu.make_async_copy(coupling.at[0], mats, mats_sem)
    mats_in.start()
    my_columns = pl.ds(pl.multiple_of(clus * panels, panels), panels)
    eval_in = pltpu.make_async_copy(evaluation.at[:, my_columns], eval_block, eval_sem)
    eval_in.start()

    small[0].wait()
    hist_in.wait()
    for l in range(lags_here):
        rows[l, 0:bodies] = hist[offsets[lag * lags_here + l]]
        for j in range(1, lags):
            hist_send[j - 1, l] = hist[offsets[lag_peers[j][2] * lags_here + l]]
    small[3].wait()
    moment_all[clus] = moment_rows[...].astype(F32)
    pl.semaphore_wait(barrier, lags - 1 + clusters - 1)

    sent = []

    def send(src, dst, sems, at, peer):
        copy = pltpu.make_async_remote_copy(
            src_ref=src, dst_ref=dst,
            send_sem=sems.at[(0,) + at], recv_sem=sems.at[(1,) + at],
            device_id=peer, device_id_type=MESH,
        )
        copy.start()
        sent.append(copy)
        return copy

    def send_history(j):
        landing = rows.at[:, pl.ds(j * bodies, bodies)]
        return send(hist_send.at[j - 1], landing, hist_sems, (j - 1,), lag_peers[j])

    hist_copies = {j: send_history(j) for j in (2, 1, 3)}
    moment_copies = [
        send(moment_all.at[clus], moment_all.at[clus], moment_sems, (r - 1,), clus_peers[r])
        for r in range(1, clusters)
    ]

    group_copies, lag_copies = [[] for _ in GROUPS], {}

    def spans(group):
        return GROUPS[group][0] * bodies, len(GROUPS[group]) * bodies

    def product(group, quad):
        if group == 0:
            weights_in[quad].wait()
        top, height = spans(group)
        total = None
        for l in range(lags_here):
            term = jnp.dot(
                rows[l, top : top + height], weights[quad, l], preferred_element_type=F32
            )
            total = term if total is None else total + term
        return total

    def begin(group):
        for j in GROUPS[group]:
            if j > 0:
                hist_copies[j].wait_recv()
        part = pl.ds(0, spans(group)[1])
        for quad in range(clusters - 1):
            value, r = product(group, quad), clusters - 1 - quad
            if r == 1:
                core_send[group, part] = value
                group_copies[group].append(
                    send(
                        core_send.at[group, part], core_recv.at[group, part],
                        core_sems, (group,), clus_peers[1],
                    )
                )
            else:
                at = (group, r - 2)
                encode(value, row_send.at[at + (part,)], row_scale.at[at])
                group_copies[group] += [
                    send(
                        row_send.at[at + (part,)], row_recv.at[at + (part,)],
                        row_sems, at, clus_peers[r],
                    ),
                    send(row_scale.at[at], row_scaled.at[at], row_scale_sems, at, clus_peers[r]),
                ]
        kept[group, part] = product(group, clusters - 1)

    def finish(group):
        for copy in group_copies[group]:
            copy.wait_recv()
        part = pl.ds(0, spans(group)[1])
        total = kept[group, part] + core_recv[group, part]
        for i in range(2):
            total = total + decode(row_recv.at[group, i, part], row_scaled.at[group, i])
        if group == 0:
            kept[0, part] = total
        for at, j in enumerate(GROUPS[group]):
            if j > 0:
                i, top = j - 1, at * bodies
                encode(total[top : top + bodies], lag_send.at[i], lag_scale.at[i])
                lag_copies[j] = (
                    send(lag_send.at[i], lag_recv.at[i], lag_sems, (i,), lag_peers[j]),
                    send(lag_scale.at[i], lag_scaled.at[i], lag_scale_sems, (i,), lag_peers[j]),
                )

    begin(0)

    small[1].wait()
    mats_in.wait()
    for copy in moment_copies:
        copy.wait_recv()
    part = None
    for l in range(lags_here):
        slot = offsets[lag * lags_here + l]
        for k in range(pairs):
            row = moment_all[pair_sources[clus, k], pl.ds(slot, 1), :]
            row = jnp.broadcast_to(row, (16, row.shape[1])).astype(BF16)
            term = lax.dot_general(
                row, mats[k, l], (((1,), (1,)), ((), ())), preferred_element_type=F32
            )
            part = term if part is None else part + term
    part_send[...] = part[0:8]
    part_copies = [
        send(part_send, part_recv.at[j - 1], part_sems, (j - 1,), lag_peers[j])
        for j in range(1, lags)
    ]

    begin(1)
    finish(0)

    local = part_send[...]
    for j in range(1, lags):
        part_copies[j - 1].wait_recv()
        local = local + part_recv[j - 1]
    local_all[clus] = local
    local_copies = [
        send(local_all.at[clus], local_all.at[clus], local_sems, (r - 1,), clus_peers[r])
        for r in range(1, clusters)
    ]

    begin(2)
    finish(1)
    finish(2)

    small[2].wait()
    eval_in.wait()
    for copy in local_copies:
        copy.wait_recv()
    expansions = local_all[...].reshape(clusters * 8, local_all.shape[2])
    far_rows[...] = jnp.dot(
        expansions, eval_block[...], precision=lax.Precision.HIGHEST, preferred_element_type=F32
    )
    for b in range(bodies):
        far[b : b + 1, :] = far_rows[pl.ds(body_cluster[lag * bodies + b] * 8, 1), :]

    total = kept[0, 0:bodies]
    for j in range(1, lags):
        for copy in lag_copies[j]:
            copy.wait_recv()
        total = total + decode(lag_recv.at[j - 1], lag_scaled.at[j - 1])
    out[...] = (total + far[...]).astype(BF16)
    for copy in sent:
        copy.wait_send()


def shards_kernel(lags, clusters, history, kernel, moments, coupling, evaluation, offsets, pair_sources, body_cluster):
    slots, bodies, panels = history.shape
    lags_here, depth, _ = kernel.shape
    terms = moments.shape[2]
    moments = moments.reshape(slots, terms)
    pairs = coupling.shape[1]
    dma = pltpu.SemaphoreType.DMA
    anywhere = pl.BlockSpec(memory_space=pl.ANY)
    vmem = pl.BlockSpec(memory_space=pltpu.VMEM)
    block, double, groups = (bodies, panels), (2 * bodies, panels), len(GROUPS)
    flops = 2 * lags * bodies * lags_here * depth * clusters * panels
    return pl.pallas_call(
        functools.partial(body, lags, clusters),
        out_shape=pltpu.VMEM(block, BF16),
        in_specs=[anywhere] * 8,
        out_specs=vmem,
        scratch_shapes=[
            pltpu.SMEM(offsets.shape, jnp.int32),
            pltpu.SMEM(pair_sources.shape, jnp.int32),
            pltpu.SMEM(body_cluster.shape, jnp.int32),
            pltpu.VMEM((slots, terms), BF16),
            pltpu.VMEM((slots,) + block, BF16),
            pltpu.VMEM((clusters, lags_here, depth, panels), BF16),
            pltpu.VMEM((pairs, lags_here, terms, terms), BF16),
            pltpu.VMEM((terms, panels), F32),
            pltpu.VMEM((lags_here, lags * bodies, panels), BF16),
            pltpu.VMEM((lags - 1, lags_here) + block, BF16),
            pltpu.VMEM((groups,) + double, F32),
            pltpu.VMEM((groups,) + double, F32),
            pltpu.VMEM((groups, 2) + double, jnp.int16),
            pltpu.VMEM((groups, 2) + double, jnp.int16),
            pltpu.VMEM((groups, 2, 8, 128), F32),
            pltpu.VMEM((groups, 2, 8, 128), F32),
            pltpu.VMEM((lags - 1,) + block, jnp.int16),
            pltpu.VMEM((lags - 1,) + block, jnp.int16),
            pltpu.VMEM((lags - 1, 8, 128), F32),
            pltpu.VMEM((lags - 1, 8, 128), F32),
            pltpu.VMEM((groups,) + double, F32),
            pltpu.VMEM((clusters, slots, terms), F32),
            pltpu.VMEM((8, terms), F32),
            pltpu.VMEM((lags - 1, 8, terms), F32),
            pltpu.VMEM((clusters, 8, terms), F32),
            pltpu.VMEM((clusters * 8, panels), F32),
            pltpu.VMEM(block, F32),
            dma((4,)), dma, dma((clusters,)), dma, dma,
            dma((2, lags - 1)), dma((2, groups)), dma((2, groups, 2)), dma((2, lags - 1)),
            dma((2, groups, 2)), dma((2, lags - 1)),
            dma((2, clusters - 1)), dma((2, lags - 1)), dma((2, clusters - 1)),
        ],
        compiler_params=pltpu.CompilerParams(
            collective_id=0, has_side_effects=True, vmem_limit_bytes=63 * 1024 * 1024
        ),
        cost_estimate=pl.CostEstimate(
            flops=flops, bytes_accessed=2 * kernel.size, transcendentals=0
        ),
    )(history, kernel, moments, coupling, evaluation, offsets, pair_sources, body_cluster)


def shards_general(history, kernel, moments, coupling, evaluation, offsets, pair_sources, body_cluster):
    lag_index = lax.axis_index("lag")
    clus_index = lax.axis_index("clus")
    clus_count = lax.axis_size("clus")
    lags_here = kernel.shape[0]
    panel_block = history.shape[2]
    body_block = history.shape[1]
    picked = jnp.take(history, offsets, axis=0)
    arrived = lax.all_to_all(picked, "lag", split_axis=0, concat_axis=1, tiled=True)
    partial_value = jnp.einsum("lbp,lpq->bq", arrived, kernel, preferred_element_type=jnp.float32)
    my_lags = lag_index * lags_here + jnp.arange(lags_here)
    my_slots = jnp.take(offsets, my_lags, axis=0)
    wanted = jnp.take(moments, my_slots, axis=0)
    source_row = lax.dynamic_index_in_dim(pair_sources, clus_index, 0, keepdims=False)
    piece = lax.all_gather(wanted, "clus", axis=1, tiled=True)
    count = piece.shape[1]
    hits = (source_row[:, None] == jnp.arange(count)[None, :]).astype(jnp.float32)
    gathered = jnp.einsum("kn,lnm->klm", hits, piece.astype(jnp.float32))
    selected = gathered.astype(jnp.bfloat16)
    local_part = jnp.einsum(
        "klmn,kln->m", coupling[0], selected, preferred_element_type=jnp.float32
    )
    owned_rows = lax.psum_scatter(partial_value, "lag", scatter_dimension=0, tiled=True)
    owned = lax.psum_scatter(owned_rows, "clus", scatter_dimension=1, tiled=True)
    cluster_ids = jnp.arange(clus_count)
    placed = (cluster_ids == clus_index).astype(jnp.float32)[:, None] * local_part[None, :]
    expansion_all = lax.psum(placed, ("clus", "lag"))
    eval_block = lax.dynamic_slice_in_dim(evaluation, clus_index * panel_block, panel_block, 1)
    far_block = jnp.dot(expansion_all, eval_block, precision=lax.Precision.HIGHEST)
    my_clusters = lax.dynamic_slice_in_dim(body_cluster, lag_index * body_block, body_block, 0)
    chooser = (my_clusters[:, None] == cluster_ids[None, :]).astype(jnp.float32)
    owned = owned + jnp.dot(chooser, far_block, precision=lax.Precision.HIGHEST)
    return owned.astype(jnp.bfloat16)


def solution(mesh):
    in_specs = (
        P(None, ("farm", "lag"), "clus"),
        P("lag", "clus", None),
        P(None, ("farm", "clus"), None),
        P("clus", None, "lag", None, None),
        P(),
        P(),
        P(),
        P(),
    )
    out_specs = P(("farm", "lag"), "clus")
    lags, clusters = mesh.shape["lag"], mesh.shape["clus"]
    if lags == 4 and clusters == 4:
        shards = functools.partial(shards_kernel, lags, clusters)
    else:
        shards = shards_general
    return jax.shard_map(shards, mesh=mesh, in_specs=in_specs, out_specs=out_specs, check_vma=False)
```
